128 devices in a mesh: row: 8 (over z_hi, x), col: 16 (over y, z_lo, core).
Axes of the slice: x: 4, y: 4, z: 4 (z_hi: 2, z_lo: 2; z = z_hi * 2 + z_lo), core: 2. Of those that a mesh axis runs over, the one named last changes fastest.
Arguments:
- pair: float32 [768, 768, 128], P('row', 'col'), may hold values from -6 to 6
- in_gain: float32 [2, 128], replicated, may hold values from 0.1 to 1.9
- in_bias: float32 [2, 128], replicated, may hold values from -0.72 to 0.72
- mid_gain: float32 [2, 128], replicated, may hold values from 0.1 to 1.9
- mid_bias: float32 [2, 128], replicated, may hold values from -3 to 3
- w_in: bfloat16 [2, 128, 512], replicated, may hold values from -0.5 to 0.5
- w_gate: bfloat16 [2, 128, 128], replicated, may hold values from -0.5 to 0.5
- w_out: bfloat16 [2, 128, 128], replicated, may hold values from -0.5 to 0.5
Outputs:
- updated: float32 [768, 768, 128], P('row', 'col')
The draws below stay inside these ranges and needn't reach their ends.
All inputs are finite; a program needn't handle non-finite values.
Results may differ from the reference program's by a relative error of at most 0.007.
Values may be sent and summed in bfloat16 or wider, within the bound.
A program may use at most 192 MiB of HBM per device.

```python
import jax
import jax.numpy as jnp
from jax import lax

CZ = 128
HID = 128
N = 768


def level_of(stream_key, shape, split, least, largest):
    def one(axis_at, parts):
        steps = jax.random.uniform(jax.random.fold_in(jax.random.fold_in(stream_key, 6), axis_at), (parts,), jnp.float32, least / len(split), largest / len(split))
        return jnp.repeat(jnp.exp(steps), shape[axis_at] // parts).reshape((-1,) + (1,) * (len(shape) - axis_at - 1))

    gain = one(*split[0])
    for cut in split[1:]:
        gain = gain * one(*cut)
    return gain


def noise(rng, dims, deviation, bound, pieces=(), dtype=jnp.bfloat16):
    entries = deviation * jax.random.normal(rng, dims, jnp.float32)
    if pieces:
        entries = entries * level_of(rng, dims, pieces, -0.22, 0.18)
    return jnp.clip(entries, -bound, bound).astype(dtype)


def setup_inputs(seed: int = 0) -> dict:
    key_list = jax.random.split(jax.random.key(seed), 9)
    pair = noise(key_list[0], (N, N, CZ), 1.0, 6.0, ((0, 8), (1, 16)), jnp.float32)
    in_gain = jnp.clip(1.0 + 0.18 * jax.random.normal(key_list[1], (2, CZ), jnp.float32), 0.1, 1.9)
    in_bias = noise(key_list[2], (2, CZ), 0.12, 0.72, (), jnp.float32)
    mid_gain = jnp.clip(1.0 + 0.18 * jax.random.normal(key_list[3], (2, HID), jnp.float32), 0.1, 1.9)
    mid_bias = noise(key_list[4], (2, HID), 0.5, 3.0, (), jnp.float32)
    w_in = noise(key_list[5], (2, CZ, 4 * HID), CZ ** -0.5, 0.5)
    w_gate = noise(key_list[6], (2, CZ, CZ), CZ ** -0.5, 0.5)
    w_out = noise(key_list[7], (2, HID, CZ), HID ** -0.5, 0.5)
    return {"pair": pair, "in_gain": in_gain, "in_bias": in_bias, "mid_gain": mid_gain, "mid_bias": mid_bias, "w_in": w_in, "w_gate": w_gate, "w_out": w_out}


epsilon = 1e-05

def layer_norm(values, gain_row, bias_row):
    centre = lax.optimization_barrier(jnp.mean(values, axis=-1, keepdims=True))
    shifted = values - centre
    spread = lax.optimization_barrier(jnp.mean(shifted * shifted, axis=-1, keepdims=True))
    return shifted * lax.rsqrt(spread + epsilon) * gain_row + bias_row

def inputs_of(pair_state, in_gain, in_bias, w_in, w_gate, layer_idx):
    normed = layer_norm(pair_state, in_gain[layer_idx], in_bias[layer_idx]).astype(jnp.bfloat16)
    projected = jnp.dot(normed, w_in[layer_idx], preferred_element_type=jnp.float32)
    width = w_in.shape[2] // 4
    left_act = (jax.nn.sigmoid(projected[..., :width]) * projected[..., width:2 * width]).astype(jnp.bfloat16)
    right_act = (jax.nn.sigmoid(projected[..., 2 * width:3 * width]) * projected[..., 3 * width:]).astype(jnp.bfloat16)
    gate_act = jax.nn.sigmoid(jnp.dot(normed, w_gate[layer_idx], preferred_element_type=jnp.float32))
    return (left_act, right_act, gate_act)

def finish(pair_state, tri_sum, gate_act, mid_gain, mid_bias, w_out, layer_idx):
    mixed_norm = layer_norm(tri_sum, mid_gain[layer_idx], mid_bias[layer_idx]).astype(jnp.bfloat16)
    return pair_state + gate_act * jnp.dot(mixed_norm, w_out[layer_idx], preferred_element_type=jnp.float32)

def reference(pair, in_gain, in_bias, mid_gain, mid_bias, w_in, w_gate, w_out):
    left_act, right_act, gate_act = inputs_of(pair, in_gain, in_bias, w_in, w_gate, 0)
    tri_sum = jnp.einsum('ikc,jkc->ijc', left_act.astype(jnp.float32), right_act.astype(jnp.float32), precision=lax.Precision.HIGHEST)
    after_out = finish(pair, tri_sum, gate_act, mid_gain, mid_bias, w_out, 0)
    left_act, right_act, gate_act = inputs_of(after_out, in_gain, in_bias, w_in, w_gate, 1)
    tri_sum = jnp.einsum('kic,kjc->ijc', left_act.astype(jnp.float32), right_act.astype(jnp.float32), precision=lax.Precision.HIGHEST)
    return finish(after_out, tri_sum, gate_act, mid_gain, mid_bias, w_out, 1)
```

```python
import functools

import jax
import jax.numpy as jnp
from jax import lax
from jax.experimental import pallas as pl
from jax.experimental.pallas import tpu as pltpu
from jax.sharding import PartitionSpec as P

epsilon = 1e-05
MESH = pl.DeviceIdType.MESH
DEVICES = 128


def place_of(step):
    row, col = lax.axis_index("row"), lax.axis_index("col")
    x, z_hi = row % 4, row // 4
    y, z_lo, core = col // 4, (col // 2) % 2, col % 2
    z = z_hi * 2 + z_lo
    x = (x + step) % 4
    y = (y + step // 4) % 4
    z = (z + step // 16) % 4
    core = (core + step // 64) % 2
    return (z // 2) * 4 + x, y * 4 + (z % 2) * 2 + core


def exchange_kernel(src, dst, send_sem, recv_sem, own_sem):
    me = lax.axis_index("row") * 16 + lax.axis_index("col")
    barrier = pltpu.get_barrier_semaphore()

    def greet(step, carry):
        pl.semaphore_signal(barrier, inc=1, device_id=place_of(step), device_id_type=MESH)
        return carry

    lax.fori_loop(1, DEVICES, greet, 0)
    own = pltpu.make_async_copy(src.at[me], dst.at[me], own_sem)
    own.start()
    pl.semaphore_wait(barrier, DEVICES - 1)

    def send(step, carry):
        target = place_of((step * 37) % DEVICES)
        pltpu.make_async_remote_copy(
            src_ref=src.at[target[0] * 16 + target[1]],
            dst_ref=dst.at[me],
            send_sem=send_sem,
            recv_sem=recv_sem,
            device_id=target,
            device_id_type=MESH,
        ).start()
        return carry

    lax.fori_loop(1, DEVICES, send, 0)
    own.wait()
    others = pl.ds(0, DEVICES - 1)
    pltpu.make_async_copy(src.at[others], src.at[others], send_sem).wait()
    pltpu.make_async_copy(dst.at[others], dst.at[others], recv_sem).wait()


def exchange(blocks, collective_id):
    return pl.pallas_call(
        exchange_kernel,
        out_shape=jax.ShapeDtypeStruct(blocks.shape, blocks.dtype),
        in_specs=[pl.BlockSpec(memory_space=pl.ANY)],
        out_specs=pl.BlockSpec(memory_space=pl.ANY),
        scratch_shapes=[pltpu.SemaphoreType.DMA] * 3,
        compiler_params=pltpu.CompilerParams(collective_id=collective_id, has_side_effects=True),
    )(blocks)


def layer_norm(values, gain_row, bias_row):
    centre = jnp.mean(values, axis=-1, keepdims=True)
    shifted = values - centre
    spread = jnp.mean(shifted * shifted, axis=-1, keepdims=True)
    return shifted * lax.rsqrt(spread + epsilon) * gain_row + bias_row


def inputs_of(pair_state, in_gain, in_bias, w_in, w_gate, layer_idx):
    normed = layer_norm(pair_state, in_gain[layer_idx], in_bias[layer_idx]).astype(jnp.bfloat16)
    projected = jnp.dot(normed, w_in[layer_idx], preferred_element_type=jnp.float32)
    width = w_in.shape[2] // 4
    left_act = (jax.nn.sigmoid(projected[..., :width]) * projected[..., width : 2 * width]).astype(
        jnp.bfloat16
    )
    right_act = (
        jax.nn.sigmoid(projected[..., 2 * width : 3 * width]) * projected[..., 3 * width :]
    ).astype(jnp.bfloat16)
    gate_act = jax.nn.sigmoid(
        jnp.dot(normed, w_gate[layer_idx], preferred_element_type=jnp.float32)
    )
    return (left_act, right_act, gate_act)


def finish(pair_state, tri_sum, gate_act, mid_gain, mid_bias, w_out, layer_idx):
    mixed_norm = layer_norm(tri_sum, mid_gain[layer_idx], mid_bias[layer_idx]).astype(jnp.bfloat16)
    return pair_state + gate_act * jnp.dot(
        mixed_norm, w_out[layer_idx], preferred_element_type=jnp.float32
    )


def whole(blocks):
    return blocks.reshape(8, 16, 96, 48).transpose(0, 2, 1, 3).reshape(768, 768)


def triangle(left_act, right_act, layer_idx):
    both = jnp.stack([left_act.reshape(4608, 128).T, right_act.reshape(4608, 128).T], axis=1)
    got = exchange(both.reshape(128, 72, 128), 2 * layer_idx).reshape(128, 2, 4608)
    left, right = whole(got[:, 0]), whole(got[:, 1])
    summed = jnp.einsum(
        "ik,jk->ij" if layer_idx == 0 else "ki,kj->ij", left, right, preferred_element_type=jnp.float32
    ).astype(jnp.bfloat16)
    blocks = summed.reshape(8, 96, 16, 48).transpose(0, 2, 1, 3).reshape(128, 36, 128)
    back = exchange(blocks, 2 * layer_idx + 1).reshape(128, 4608)
    return back.T.reshape(96, 48, 128).astype(jnp.float32)


def local(pair, in_gain, in_bias, mid_gain, mid_bias, w_in, w_gate, w_out):
    for layer_idx in range(2):
        left_act, right_act, gate_act = inputs_of(pair, in_gain, in_bias, w_in, w_gate, layer_idx)
        tri_sum = triangle(left_act, right_act, layer_idx)
        pair = finish(pair, tri_sum, gate_act, mid_gain, mid_bias, w_out, layer_idx)
    return pair


def solution(mesh):
    return jax.shard_map(
        local,
        mesh=mesh,
        in_specs=(P("row", "col", None), P(), P(), P(), P(), P(), P(), P()),
        out_specs=P("row", "col", None),
        check_vma=False,
    )
```

```python
import jax
import jax.numpy as jnp
from jax import lax
from jax.experimental import pallas as pl
from jax.experimental.pallas import tpu as pltpu
from jax.sharding import PartitionSpec as P

epsilon = 1e-05
MESH = pl.DeviceIdType.MESH
DEVICES = 128
F32, BF16 = jnp.float32, jnp.bfloat16
STRIDE = 73


def coordinates():
    row, col = lax.axis_index("row"), lax.axis_index("col")
    return row % 4, col // 4, (row // 4) * 2 + (col // 2) % 2, col % 2


def device_at(x, y, z, core):
    return (z // 2) * 4 + x, y * 4 + (z % 2) * 2 + core


def peer(group, member):
    x, y, z, core = coordinates()
    gx, gy, gz = (x + group) % 2, (y + group // 2) % 2, (z + group // 4) % 2
    mx, my, mz = (x // 2 + member) % 2, (y // 2 + member // 2) % 2, (z // 2 + member // 4) % 2
    core = (core + member // 8) % 2
    channel = (gx + gy * 2 + gz * 4) * 16 + mx + my * 2 + mz * 4 + core * 8
    return device_at(mx * 2 + gx, my * 2 + gy, mz * 2 + gz, core), channel


def sigmoid(values):
    return 0.5 * jnp.tanh(0.5 * values) + 0.5


def norm_columns(values, gain, bias):
    centre = jnp.mean(values, axis=0, keepdims=True)
    shifted = values - centre
    spread = jnp.mean(shifted * shifted, axis=0, keepdims=True)
    return (shifted * lax.rsqrt(spread + epsilon) * gain + bias).astype(BF16)


def turn(blocks):
    lane = lax.broadcasted_iota(jnp.int32, blocks[0].shape, 1)
    first, even = lane < 64, lane % 64 < 32
    a0, a1, a2, a3 = blocks
    b0, b2 = jnp.where(first, a0, pltpu.roll(a2, 64, 1)), jnp.where(first, pltpu.roll(a0, 64, 1), a2)
    b1, b3 = jnp.where(first, a1, pltpu.roll(a3, 64, 1)), jnp.where(first, pltpu.roll(a1, 64, 1), a3)
    c0, c1 = jnp.where(even, b0, pltpu.roll(b1, 32, 1)), jnp.where(even, pltpu.roll(b0, 96, 1), b1)
    c2, c3 = jnp.where(even, b2, pltpu.roll(b3, 32, 1)), jnp.where(even, pltpu.roll(b2, 96, 1), b3)
    return c0, c1, c2, c3


def kernel(
    pair, in_gain, in_bias, mid_gain, mid_bias, w_in, w_gate, w_out, out,
    rows, state, gate, normed, staged, spread_out, outgoing, incoming, sums_out, sums_in,
    left, right, left16, summed, piece, weights, gate_t, out_t, columns,
    copy_sem, own_sem, send_sem, recv_sem,
):
    me_row, me_col = lax.axis_index("row"), lax.axis_index("col")
    me = me_row * 16 + me_col
    barrier = pltpu.get_barrier_semaphore()
    load = pltpu.make_async_copy(pair, rows, copy_sem)
    load.start()

    def greet(step, carry):
        pl.semaphore_signal(barrier, inc=1, device_id=peer(step // 16, step % 16)[0], device_id_type=MESH)
        return carry

    lax.fori_loop(1, DEVICES, greet, 0)

    for u in range(2):
        for part in range(4):
            block = w_in[u, :, part * 128 : (part + 1) * 128].astype(F32).T.astype(BF16)
            for group in range(8):
                weights[u, group, part * 16 : (part + 1) * 16, :] = block[group * 16 : (group + 1) * 16]
        gate_t[u] = w_gate[u].astype(F32).T.astype(BF16)
        out_t[u] = w_out[u].astype(F32).T.astype(BF16)
        for at, row in enumerate((in_gain, in_bias, mid_gain, mid_bias)):
            columns[u, at] = jnp.broadcast_to(row[u : u + 1, :], (128, 128)).T

    load.wait()
    whole_sum = summed.reshape(768, 768)

    def token_rows(tile, quarter):
        start = (tile // 12) * 1536 + tile % 12 + quarter * 12
        return pl.ds(start, 32, stride=48)

    def enter(pair_of, carry):
        halves = []
        for half in range(2):
            tile = pair_of * 2 + half
            tokens = jnp.concatenate([rows[token_rows(tile, q), :] for q in range(4)], axis=0)
            values = tokens.T
            state[tile] = values
            halves.append(norm_columns(values, columns[0, 0], columns[0, 1]))
        normed[pair_of] = jnp.concatenate(halves, axis=1)
        return carry

    lax.fori_loop(0, 18, enter, 0)

    for u in range(2):
        def group_step(group, carry):
            (_, _), first_channel = peer(group, 0)
            which = first_channel // 16

            def project(pair_of, inner):
                projected = jnp.dot(weights[u, which], normed[pair_of], preferred_element_type=F32)
                for side in range(2):
                    at = side * 32
                    acts = sigmoid(projected[at : at + 16]) * projected[at + 16 : at + 32]
                    for octet in range(2):
                        for half in range(2):
                            start = octet * 8 * STRIDE + side * 36 + pair_of * 2 + half
                            staged[pl.ds(start, 8, stride=STRIDE), :] = acts[
                                octet * 8 : octet * 8 + 8, half * 128 : half * 128 + 128
                            ]
                return inner

            lax.fori_loop(0, 18, project, 0)

            def send(member, inner):
                target, channel = peer(group, member)
                outgoing[channel] = staged[pl.ds((channel % 16) * STRIDE, 72), :].astype(BF16)

                @pl.when(group + member > 0)
                def _():
                    pltpu.make_async_remote_copy(
                        src_ref=outgoing.at[channel], dst_ref=incoming.at[me],
                        send_sem=send_sem.at[2 * u], recv_sem=recv_sem.at[2 * u],
                        device_id=target, device_id_type=MESH,
                    ).start()

                @pl.when(group + member == 0)
                def _():
                    pltpu.make_async_copy(outgoing.at[channel], incoming.at[me], own_sem.at[2 * u]).start()

                return inner

            if u == 0:
                @pl.when(group == 0)
                def _():
                    pl.semaphore_wait(barrier, DEVICES - 1)

            lax.fori_loop(0, 16, send, 0)
            return carry

        lax.fori_loop(0, 8, group_step, 0)

        def gates(pair_of, carry):
            value = sigmoid(jnp.dot(gate_t[u], normed[pair_of], preferred_element_type=F32))
            gate[pair_of * 2] = value[:, :128]
            gate[pair_of * 2 + 1] = value[:, 128:]
            return carry

        lax.fori_loop(0, 18, gates, 0)

        others = pl.ds(0, DEVICES - 1)
        pltpu.make_async_copy(outgoing.at[0], incoming.at[0], own_sem.at[2 * u]).wait()
        pltpu.make_async_copy(incoming.at[others], incoming.at[others], recv_sem.at[2 * u]).wait()

        def gather(s, carry):
            for z_hi in range(2):
                turned = turn([incoming[(z_hi * 4 + x) * 16 + s].astype(F32) for x in range(4)])
                for quarter in range(4):
                    for third in range(3):
                        lanes = pl.ds((z_hi * 3 + third) * 128, 128)
                        to = pl.ds(quarter * 12, 12)
                        left[s, to, lanes] = turned[quarter][third * 12 : third * 12 + 12]
                        right[s, to, lanes] = turned[quarter][36 + third * 12 : 48 + third * 12]
            return carry

        lax.fori_loop(0, 16, gather, 0)

        if u == 0:
            left16[...] = left[...].reshape(768, 768).astype(BF16)

            for z_hi in range(2):
                for third in range(3):
                    at = (z_hi * 3 + third) * 128
                    turned = right[:, :, at : at + 128].reshape(768, 128).T.astype(BF16)
                    product = jnp.dot(turned, left16[...], preferred_element_type=F32)
                    for x in range(4):
                        to = (z_hi * 4 + x) * 96 + third * 32
                        whole_sum[to : to + 32, :] = product[x * 32 : x * 32 + 32]
        else:
            flat = left.reshape(768, 768)
            for z_hi in range(2):
                for third in range(3):
                    for x in range(4):
                        at = (z_hi * 4 + x) * 96 + third * 32
                        to = (z_hi * 3 + third) * 128 + x * 32
                        left16[to : to + 32, :] = flat[at : at + 32, :].astype(BF16)
            flat = right.reshape(768, 768)
            for at in range(0, 768, 128):
                whole_sum[at : at + 128, :] = lax.dot_general(
                    flat[at : at + 128, :].astype(BF16), left16[...], (((1,), (1,)), ((), ())),
                    preferred_element_type=F32,
                )

        if u == 1:
            pltpu.make_async_copy(sums_out.at[others], sums_out.at[others], send_sem.at[1]).wait()

        def give_back(step, carry):
            s = (me_col + step * 5) % 16
            for z_hi in range(2):
                for quarter in range(4):
                    for third in range(3):
                        piece[quarter, third * 12 : third * 12 + 12, :] = summed[
                            s, pl.ds(quarter * 12, 12), pl.ds((z_hi * 3 + third) * 128, 128)
                        ]
                turned = turn([piece[quarter] for quarter in range(4)])
                for x in range(4):
                    row = z_hi * 4 + x
                    to = row * 16 + s
                    sums_out[to] = turned[x].astype(BF16)

                    @pl.when(to != me)
                    def _():
                        pltpu.make_async_remote_copy(
                            src_ref=sums_out.at[to], dst_ref=sums_in.at[peer(0, 0)[1]],
                            send_sem=send_sem.at[2 * u + 1], recv_sem=recv_sem.at[2 * u + 1],
                            device_id=(row, s), device_id_type=MESH,
                        ).start()

                    @pl.when(to == me)
                    def _():
                        pltpu.make_async_copy(
                            sums_out.at[to], sums_in.at[peer(0, 0)[1]], own_sem.at[2 * u + 1]
                        ).start()

            return carry

        lax.fori_loop(0, 16, give_back, 0)

        pltpu.make_async_copy(sums_out.at[0], sums_in.at[0], own_sem.at[2 * u + 1]).wait()
        pltpu.make_async_copy(sums_in.at[others], sums_in.at[others], recv_sem.at[2 * u + 1]).wait()
        pltpu.make_async_copy(outgoing.at[others], outgoing.at[others], send_sem.at[2 * u]).wait()

        def widen(channel, carry):
            spread_out[channel, 0:36, :] = sums_in[channel].astype(F32)
            return carry

        lax.fori_loop(0, DEVICES, widen, 0)
        flat_sums = spread_out.reshape(128 * 40, 128)

        def finish(pair_of, carry):
            mixed = []
            for half in range(2):
                values = flat_sums[pl.ds(pair_of * 2 + half, 128, stride=40), :]
                mixed.append(norm_columns(values, columns[u, 2], columns[u, 3]))
            update = jnp.dot(out_t[u], jnp.concatenate(mixed, axis=1), preferred_element_type=F32)
            halves = []
            for half in range(2):
                tile = pair_of * 2 + half
                values = state[tile] + gate[tile] * update[:, half * 128 : half * 128 + 128]
                if u == 0:
                    state[tile] = values
                    halves.append(norm_columns(values, columns[1, 0], columns[1, 1]))
                else:
                    tokens = values.T
                    for q in range(4):
                        rows[token_rows(tile, q), :] = tokens[q * 32 : q * 32 + 32]
            if u == 0:
                normed[pair_of] = jnp.concatenate(halves, axis=1)
            return carry

        lax.fori_loop(0, 18, finish, 0)

    pltpu.make_async_copy(sums_out.at[others], sums_out.at[others], send_sem.at[3]).wait()
    store = pltpu.make_async_copy(rows, out, copy_sem)
    store.start()
    store.wait()


def local(pair, *parameters):
    vmem, anywhere = pl.BlockSpec(memory_space=pltpu.VMEM), pl.BlockSpec(memory_space=pl.ANY)
    done = pl.pallas_call(
        kernel,
        out_shape=jax.ShapeDtypeStruct((4608, 128), F32),
        in_specs=[anywhere] + [vmem] * 7,
        out_specs=anywhere,
        scratch_shapes=[
            pltpu.VMEM((4608, 128), F32),
            pltpu.VMEM((36, 128, 128), F32),
            pltpu.VMEM((36, 128, 128), F32),
            pltpu.VMEM((18, 128, 256), BF16),
            pltpu.VMEM((16 * STRIDE + 8, 128), F32),
            pltpu.VMEM((128, 40, 128), F32),
            pltpu.VMEM((128, 72, 128), BF16),
            pltpu.VMEM((128, 72, 128), BF16),
            pltpu.VMEM((128, 36, 128), BF16),
            pltpu.VMEM((128, 36, 128), BF16),
            pltpu.VMEM((16, 48, 768), F32),
            pltpu.VMEM((16, 48, 768), F32),
            pltpu.VMEM((768, 768), BF16),
            pltpu.VMEM((16, 48, 768), F32),
            pltpu.VMEM((4, 36, 128), F32),
            pltpu.VMEM((2, 8, 64, 128), BF16),
            pltpu.VMEM((2, 128, 128), BF16),
            pltpu.VMEM((2, 128, 128), BF16),
            pltpu.VMEM((2, 4, 128, 128), F32),
            pltpu.SemaphoreType.DMA,
            pltpu.SemaphoreType.DMA((4,)),
            pltpu.SemaphoreType.DMA((4,)),
            pltpu.SemaphoreType.DMA((4,)),
        ],
        compiler_params=pltpu.CompilerParams(
            collective_id=0, has_side_effects=True, vmem_limit_bytes=56 * 2**20
        ),
    )(pair.reshape(4608, 128), *parameters)
    return done.reshape(96, 48, 128)


def solution(mesh):
    return jax.shard_map(
        local,
        mesh=mesh,
        in_specs=(P("row", "col", None), P(), P(), P(), P(), P(), P(), P()),
        out_specs=P("row", "col", None),
        check_vma=False,
    )
```

```python
import jax
import jax.numpy as jnp
from jax import lax
from jax.experimental import pallas as pl
from jax.experimental.pallas import tpu as pltpu
from jax.sharding import PartitionSpec as P

epsilon = 1e-05
MESH = pl.DeviceIdType.MESH
DEVICES = 128
F32, BF16 = jnp.float32, jnp.bfloat16
STRIDE = 73
WIDE = 41


def add_mod(value, offset, size):
    return lax.rem(value + offset, size)


def device_at(x, y, z, core):
    return lax.div(z, 2) * 4 + x, y * 4 + lax.rem(z, 2) * 2 + core


def sigmoid(values):
    return 0.5 * jnp.tanh(0.5 * values) + 0.5


def norm_columns(values, gain, bias):
    centre = jnp.mean(values, axis=0, keepdims=True)
    shifted = values - centre
    spread = jnp.mean(shifted * shifted, axis=0, keepdims=True)
    return (shifted * lax.rsqrt(spread + epsilon) * gain + bias).astype(BF16)


def turn(blocks):
    lane = lax.broadcasted_iota(jnp.int32, blocks[0].shape, 1)
    first, even = lane < 64, lane % 64 < 32
    a0, a1, a2, a3 = blocks
    b0, b2 = jnp.where(first, a0, pltpu.roll(a2, 64, 1)), jnp.where(first, pltpu.roll(a0, 64, 1), a2)
    b1, b3 = jnp.where(first, a1, pltpu.roll(a3, 64, 1)), jnp.where(first, pltpu.roll(a1, 64, 1), a3)
    c0, c1 = jnp.where(even, b0, pltpu.roll(b1, 32, 1)), jnp.where(even, pltpu.roll(b0, 96, 1), b1)
    c2, c3 = jnp.where(even, b2, pltpu.roll(b3, 32, 1)), jnp.where(even, pltpu.roll(b2, 96, 1), b3)
    return c0, c1, c2, c3


def kernel(
    pair, in_gain_h, in_bias_h, mid_gain_h, mid_bias_h, w_in_h, w_gate_h, w_out_h, out,
    in_gain, in_bias, mid_gain, mid_bias, w_in, w_gate, w_out,
    rows, state, gate, normed, staged, widened, outgoing, incoming, sums_out, sums_in,
    slab_left, slab_right, left16, right16, right_t, summed, piece, weights, gate_t, out_t, columns,
    copy_sem, param_sem, own_sem, send_sem, recv_sem, sums_sem, plane_sem,
):
    row, col = lax.axis_index("row"), lax.axis_index("col")
    me = row * 16 + col
    x, z_hi = lax.rem(row, 4), lax.div(row, 4)
    y, z_lo, core = lax.div(col, 4), lax.rem(lax.div(col, 2), 2), lax.rem(col, 2)
    z = z_hi * 2 + z_lo
    y_lo, y_hi = lax.rem(y, 2), lax.div(y, 2)
    my_channel = (y_lo + z_lo * 2 + core * 4) * 16 + x + y_hi * 4 + z_hi * 8

    loads = [
        pltpu.make_async_copy(pair.at[pl.ds(i * 1536, 1536)], rows.at[pl.ds(i * 1536, 1536)], copy_sem.at[i])
        for i in range(3)
    ]
    parameters = [
        pltpu.make_async_copy(from_hbm, to, param_sem.at[i])
        for i, (from_hbm, to) in enumerate(
            (
                (in_gain_h, in_gain), (in_bias_h, in_bias), (w_in_h, w_in), (mid_gain_h, mid_gain),
                (mid_bias_h, mid_bias), (w_gate_h, w_gate), (w_out_h, w_out),
            )
        )
    ]
    for load in parameters[:3] + loads + parameters[3:]:
        load.start()

    along_x = [device_at(add_mod(x, i, 4), y, z, core) for i in range(1, 4)]
    along_y = [device_at(x, add_mod(y, i, 4), z, core) for i in range(1, 4)]
    along_z = [device_at(x, y, add_mod(z, i, 4), core) for i in range(1, 4)]
    other_core = [device_at(x, y, z, 1 - core)]
    barrier = pltpu.get_barrier_semaphore()

    def tell(semaphore, devices):
        for device in devices:
            pl.semaphore_signal(semaphore, inc=1, device_id=device, device_id_type=MESH)

    tell(barrier, along_x + along_y + along_z + other_core)

    def prepare(u, what):
        if what == "in":
            for at, source in enumerate((in_gain, in_bias)):
                columns[u, at] = jnp.broadcast_to(source[u : u + 1, :], (128, 128)).T
            for part in range(4):
                block = w_in[u, :, part * 128 : (part + 1) * 128].astype(F32).T.astype(BF16)
                for group in range(8):
                    weights[u, group, part * 16 : (part + 1) * 16, :] = block[group * 16 : (group + 1) * 16]
        else:
            gate_t[u] = w_gate[u].astype(F32).T.astype(BF16)
            out_t[u] = w_out[u].astype(F32).T.astype(BF16)
            for at, source in enumerate((mid_gain, mid_bias)):
                columns[u, 2 + at] = jnp.broadcast_to(source[u : u + 1, :], (128, 128)).T

    for load in parameters[:3]:
        load.wait()
    prepare(0, "in")

    def token_rows(tile, quarter):
        start = lax.div(tile, 12) * 1536 + lax.rem(tile, 12) + quarter * 12
        return pl.ds(start, 32, stride=48)

    def enter(pair_of, carry):
        halves = []
        for half in range(2):
            tile = pair_of * 2 + half
            tokens = jnp.concatenate([rows[token_rows(tile, q), :] for q in range(4)], axis=0)
            values = tokens.T
            state[tile] = values
            halves.append(norm_columns(values, columns[0, 0], columns[0, 1]))
        normed[pair_of] = jnp.concatenate(halves, axis=1)
        return carry

    loads[0].wait()
    pl.semaphore_wait(barrier, 10)
    tell(plane_sem.at[0], along_y)
    lax.fori_loop(0, 6, enter, 0, unroll=2)
    loads[1].wait()
    pl.semaphore_wait(plane_sem.at[0], 3)
    tell(plane_sem.at[1], along_z)
    lax.fori_loop(6, 12, enter, 0, unroll=2)
    loads[2].wait()
    pl.semaphore_wait(plane_sem.at[1], 3)
    tell(plane_sem.at[2], other_core)
    lax.fori_loop(12, 18, enter, 0, unroll=2)

    others = pl.ds(0, DEVICES - 1)
    slab_left[96:128, :] = jnp.zeros((32, 768), F32)
    slab_right[96:128, :] = jnp.zeros((32, 768), F32)

    for u in range(2):
        def group_step(group, carry):
            to_y, to_z = add_mod(y_lo, group, 2), add_mod(z_lo, lax.div(group, 2), 2)
            to_core = add_mod(core, lax.div(group, 4), 2)
            which = to_y + to_z * 2 + to_core * 4

            def project(pair_of, inner):
                projected = jnp.dot(weights[u, which], normed[pair_of], preferred_element_type=F32)
                for side in range(2):
                    at = side * 32
                    acts = sigmoid(projected[at : at + 16]) * projected[at + 16 : at + 32]
                    for octet in range(2):
                        for half in range(2):
                            start = octet * 8 * STRIDE + side * 36 + pair_of * 2 + half
                            staged[pl.ds(start, 8, stride=STRIDE), :] = acts[
                                octet * 8 : octet * 8 + 8, half * 128 : half * 128 + 128
                            ]
                return inner

            lax.fori_loop(0, 18, project, 0, unroll=6)

            if u == 0:
                @pl.when(group == 0)
                def _():
                    pl.semaphore_wait(plane_sem.at[2], 1)

            def send(member, inner):
                at_x = add_mod(x, member, 4)
                at_y, at_z = add_mod(y_hi, lax.div(member, 4), 2), add_mod(z_hi, lax.div(member, 8), 2)
                place = at_x + at_y * 4 + at_z * 8
                channel = which * 16 + place
                outgoing[channel] = staged[pl.ds(place * STRIDE, 72), :].astype(BF16)

                @pl.when(group + member > 0)
                def _():
                    pltpu.make_async_remote_copy(
                        src_ref=outgoing.at[channel], dst_ref=incoming.at[me],
                        send_sem=send_sem.at[2 * u], recv_sem=recv_sem.at[u * 8 + group],
                        device_id=(at_z * 4 + at_x, at_y * 8 + to_y * 4 + to_z * 2 + to_core),
                        device_id_type=MESH,
                    ).start()

                @pl.when(group + member == 0)
                def _():
                    pltpu.make_async_copy(outgoing.at[channel], incoming.at[me], own_sem.at[2 * u]).start()

                return inner

            lax.fori_loop(0, 16, send, 0, unroll=4)
            return carry

        lax.fori_loop(0, 8, group_step, 0)

        if u == 0:
            for load in parameters[3:]:
                load.wait()
            prepare(0, "out")
            prepare(1, "in")
            prepare(1, "out")

        def gates(pair_of, carry):
            value = sigmoid(jnp.dot(gate_t[u], normed[pair_of], preferred_element_type=F32))
            gate[pair_of * 2] = value[:, :128]
            gate[pair_of * 2 + 1] = value[:, 128:]
            return carry

        lax.fori_loop(0, 18, gates, 0, unroll=2)

        pltpu.make_async_copy(outgoing.at[0], incoming.at[0], own_sem.at[2 * u]).wait()

        def gather(group, carry):
            @pl.when(group == 0)
            def _():
                part = incoming.at[pl.ds(0, 15)]
                pltpu.make_async_copy(part, part, recv_sem.at[u * 8]).wait()

            @pl.when(group > 0)
            def _():
                part = incoming.at[pl.ds(0, 16)]
                pltpu.make_async_copy(part, part, recv_sem.at[u * 8 + group]).wait()

            from_y, from_z = add_mod(y_lo, group, 2), add_mod(z_lo, lax.div(group, 2), 2)
            from_core = add_mod(core, lax.div(group, 4), 2)
            column = from_y * 4 + from_z * 2 + from_core
            for h in range(2):
                for hi in range(2):
                    turned = turn(
                        [incoming[(hi * 4 + at) * 16 + h * 8 + column].astype(F32) for at in range(4)]
                    )
                    for quarter in range(4):
                        for third in range(3):
                            lanes = pl.ds((hi * 3 + third) * 128, 128)
                            to = pl.ds(h * 48 + quarter * 12, 12)
                            slab_left[to, lanes] = turned[quarter][third * 12 : third * 12 + 12]
                            slab_right[to, lanes] = turned[quarter][36 + third * 12 : 48 + third * 12]
            if u == 0:
                left16[group] = slab_left[...].astype(BF16)
                for hi in range(2):
                    for third in range(3):
                        lanes = pl.ds((hi * 3 + third) * 128, 128)
                        flipped = slab_right[:, lanes].T.astype(BF16)
                        for at in range(4):
                            right_t[
                                pl.ds((hi * 4 + at) * 96 + third * 32, 32),
                                pl.ds(pl.multiple_of(group * 128, 128), 128),
                            ] = flipped[at * 32 : at * 32 + 32]
            else:
                for h in range(2):
                    right16[h * 8 + column] = slab_right[h * 48 : h * 48 + 48, :].astype(BF16)
                    for part in range(3):
                        sixth = from_core * 3 + part
                        to = h * 384 + lax.div(sixth, 2) * 128 + (from_y * 2 + from_z) * 32 + lax.rem(sixth, 2) * 16
                        at = h * 48 + part * 16
                        left16.reshape(1024, 768)[pl.ds(pl.multiple_of(to, 16), 16), :] = slab_left[
                            at : at + 16, :
                        ].astype(BF16)
            return carry

        lax.fori_loop(0, 8, gather, 0)

        if u == 1:
            pltpu.make_async_copy(sums_out.at[others], sums_out.at[others], send_sem.at[1]).wait()

        def give_back(step, carry):
            turn_y = lax.div(step, 2)
            to_y = add_mod(y, turn_y + lax.div(turn_y, 2) * (5 - 2 * turn_y), 4)
            to_z = add_mod(z_lo, step, 2)
            pair_at = to_y * 2 + to_z
            rows_at = pl.ds(pl.multiple_of(pair_at * 96, 96), 96)
            if u == 0:
                product = jnp.dot(right_t[rows_at, :], left16.reshape(1024, 768)[...], preferred_element_type=F32)
            else:
                product = lax.dot_general(
                    right16.reshape(768, 768)[rows_at, :], left16.reshape(1024, 768)[0:768, :],
                    (((1,), (1,)), ((), ())), preferred_element_type=F32,
                )
            summed[...] = product
            for to_core in range(2):
                s = pair_at * 2 + to_core
                for hi in range(2):
                    for quarter in range(4):
                        for third in range(3):
                            piece[quarter, third * 12 : third * 12 + 12, :] = summed[
                                pl.ds(to_core * 48 + quarter * 12, 12), pl.ds((hi * 3 + third) * 128, 128)
                            ]
                    turned = turn([piece[quarter] for quarter in range(4)])
                    for at in range(4):
                        to_row = hi * 4 + at
                        to = to_row * 16 + s
                        sums_out[to] = turned[at].astype(BF16)

                        @pl.when(to != me)
                        def _():
                            pltpu.make_async_remote_copy(
                                src_ref=sums_out.at[to], dst_ref=sums_in.at[my_channel],
                                send_sem=send_sem.at[2 * u + 1], recv_sem=sums_sem.at[u],
                                device_id=(to_row, s), device_id_type=MESH,
                            ).start()

                        @pl.when(to == me)
                        def _():
                            pltpu.make_async_copy(
                                sums_out.at[to], sums_in.at[my_channel], own_sem.at[2 * u + 1]
                            ).start()

            return carry

        lax.fori_loop(0, 8, give_back, 0)

        pltpu.make_async_copy(sums_out.at[0], sums_in.at[0], own_sem.at[2 * u + 1]).wait()
        pltpu.make_async_copy(sums_in.at[others], sums_in.at[others], sums_sem.at[u]).wait()
        pltpu.make_async_copy(outgoing.at[others], outgoing.at[others], send_sem.at[2 * u]).wait()

        def widen(channel, carry):
            widened[pl.ds(channel * WIDE, 36), :] = sums_in[channel].astype(F32)
            return carry

        lax.fori_loop(0, DEVICES, widen, 0, unroll=8)

        def finish(pair_of, carry):
            mixed = []
            for half in range(2):
                values = widened[pl.ds(pair_of * 2 + half, 128, stride=WIDE), :]
                mixed.append(norm_columns(values, columns[u, 2], columns[u, 3]))
            update = jnp.dot(out_t[u], jnp.concatenate(mixed, axis=1), preferred_element_type=F32)
            halves = []
            for half in range(2):
                tile = pair_of * 2 + half
                values = state[tile] + gate[tile] * update[:, half * 128 : half * 128 + 128]
                if u == 0:
                    state[tile] = values
                    halves.append(norm_columns(values, columns[1, 0], columns[1, 1]))
                else:
                    tokens = values.T
                    for q in range(4):
                        rows[token_rows(tile, q), :] = tokens[q * 32 : q * 32 + 32]
            if u == 0:
                normed[pair_of] = jnp.concatenate(halves, axis=1)
            return carry

        if u == 0:
            lax.fori_loop(0, 18, finish, 0, unroll=2)
        else:
            stores = []
            for i in range(3):
                lax.fori_loop(i * 6, i * 6 + 6, finish, 0, unroll=2)
                stores.append(
                    pltpu.make_async_copy(
                        rows.at[pl.ds(i * 1536, 1536)], out.at[pl.ds(i * 1536, 1536)], copy_sem.at[i]
                    )
                )
                stores[-1].start()

    pltpu.make_async_copy(sums_out.at[others], sums_out.at[others], send_sem.at[3]).wait()
    for store in stores:
        store.wait()


def local(pair, *parameters):
    anywhere = pl.BlockSpec(memory_space=pl.ANY)
    done = pl.pallas_call(
        kernel,
        out_shape=jax.ShapeDtypeStruct((4608, 128), F32),
        in_specs=[anywhere] * 8,
        out_specs=anywhere,
        scratch_shapes=[pltpu.VMEM(p.shape, p.dtype) for p in parameters] + [
            pltpu.VMEM((4608, 128), F32),
            pltpu.VMEM((36, 128, 128), F32),
            pltpu.VMEM((36, 128, 128), F32),
            pltpu.VMEM((18, 128, 256), BF16),
            pltpu.VMEM((16 * STRIDE + 8, 128), F32),
            pltpu.VMEM((128 * WIDE, 128), F32),
            pltpu.VMEM((128, 72, 128), BF16),
            pltpu.VMEM((128, 72, 128), BF16),
            pltpu.VMEM((128, 36, 128), BF16),
            pltpu.VMEM((128, 36, 128), BF16),
            pltpu.VMEM((128, 768), F32),
            pltpu.VMEM((128, 768), F32),
            pltpu.VMEM((8, 128, 768), BF16),
            pltpu.VMEM((16, 48, 768), BF16),
            pltpu.VMEM((768, 1024), BF16),
            pltpu.VMEM((96, 768), F32),
            pltpu.VMEM((4, 36, 128), F32),
            pltpu.VMEM((2, 8, 64, 128), BF16),
            pltpu.VMEM((2, 128, 128), BF16),
            pltpu.VMEM((2, 128, 128), BF16),
            pltpu.VMEM((2, 4, 128, 128), F32),
            pltpu.SemaphoreType.DMA((3,)),
            pltpu.SemaphoreType.DMA((7,)),
            pltpu.SemaphoreType.DMA((4,)),
            pltpu.SemaphoreType.DMA((4,)),
            pltpu.SemaphoreType.DMA((16,)),
            pltpu.SemaphoreType.DMA((2,)),
            pltpu.SemaphoreType.REGULAR((3,)),
        ],
        compiler_params=pltpu.CompilerParams(
            collective_id=0, has_side_effects=True, vmem_limit_bytes=56 * 2**20
        ),
    )(pair.reshape(4608, 128), *parameters)
    return done.reshape(96, 48, 128)


def solution(mesh):
    return jax.shard_map(
        local,
        mesh=mesh,
        in_specs=(P("row", "col", None), P(), P(), P(), P(), P(), P(), P()),
        out_specs=P("row", "col", None),
        check_vma=False,
    )
```

```python
import jax
import jax.numpy as jnp
from jax import lax
from jax.experimental import pallas as pl
from jax.experimental.pallas import tpu as pltpu
from jax.sharding import PartitionSpec as P

epsilon = 1e-05
MESH = pl.DeviceIdType.MESH
DEVICES = 128
F32, BF16 = jnp.float32, jnp.bfloat16
STRIDE = 41
WIDE = 41
FIRST_ROW, ROWS = (0, 16), (16, 20)
SEGMENTS = (((0, 0, 0, 12), (12, 1, 0, 4)), ((0, 1, 4, 8), (8, 2, 0, 12)))


def add_mod(value, offset, size):
    return lax.rem(value + offset, size)


def device_at(x, y, z, core):
    return lax.div(z, 2) * 4 + x, y * 4 + lax.rem(z, 2) * 2 + core


def sigmoid(values):
    return 0.5 * jnp.tanh(0.5 * values) + 0.5


def norm_columns(values, gain, bias):
    centre = jnp.mean(values, axis=0, keepdims=True)
    shifted = values - centre
    spread = jnp.mean(shifted * shifted, axis=0, keepdims=True)
    return (shifted * lax.rsqrt(spread + epsilon) * gain + bias).astype(BF16)


def turn(blocks):
    lane = lax.broadcasted_iota(jnp.int32, blocks[0].shape, 1)
    first, even = lane < 64, lane % 64 < 32
    a0, a1, a2, a3 = blocks
    b0, b2 = jnp.where(first, a0, pltpu.roll(a2, 64, 1)), jnp.where(first, pltpu.roll(a0, 64, 1), a2)
    b1, b3 = jnp.where(first, a1, pltpu.roll(a3, 64, 1)), jnp.where(first, pltpu.roll(a1, 64, 1), a3)
    c0, c1 = jnp.where(even, b0, pltpu.roll(b1, 32, 1)), jnp.where(even, pltpu.roll(b0, 96, 1), b1)
    c2, c3 = jnp.where(even, b2, pltpu.roll(b3, 32, 1)), jnp.where(even, pltpu.roll(b2, 96, 1), b3)
    return c0, c1, c2, c3


def kernel(
    pair, in_gain_h, in_bias_h, mid_gain_h, mid_bias_h, w_in_h, w_gate_h, w_out_h, out,
    in_gain, in_bias, mid_gain, mid_bias, w_in, w_gate, w_out,
    rows, state, gate, normed, staged, widened, outgoing0, outgoing1, incoming0, incoming1,
    sums_out0, sums_out1, sums_in0, sums_in1,
    slab_left, slab_right, left16, right16, right_t, summed0, summed1, piece, weights, gate_t, out_t, columns,
    copy_sem, param_sem, own_sem, own_sums_sem, send_sem, sums_send_sem, recv_sem, sums_sem, plane_sem,
):
    row, col = lax.axis_index("row"), lax.axis_index("col")
    me = row * 16 + col
    x, z_hi = lax.rem(row, 4), lax.div(row, 4)
    y, z_lo, core = lax.div(col, 4), lax.rem(lax.div(col, 2), 2), lax.rem(col, 2)
    z = z_hi * 2 + z_lo
    y_lo, y_hi = lax.rem(y, 2), lax.div(y, 2)
    my_channel = (y_lo + z_lo * 2 + core * 4) * 16 + x + y_hi * 4 + z_hi * 8

    loads = [
        pltpu.make_async_copy(pair.at[pl.ds(i * 1536, 1536)], rows.at[pl.ds(i * 1536, 1536)], copy_sem.at[i])
        for i in range(3)
    ]
    parameters = [
        pltpu.make_async_copy(from_hbm, to, param_sem.at[i])
        for i, (from_hbm, to) in enumerate(
            (
                (in_gain_h, in_gain), (in_bias_h, in_bias), (w_in_h, w_in), (mid_gain_h, mid_gain),
                (mid_bias_h, mid_bias), (w_gate_h, w_gate), (w_out_h, w_out),
            )
        )
    ]
    for load in parameters[:3] + loads + parameters[3:]:
        load.start()

    outgoing, incoming = (outgoing0, outgoing1), (incoming0, incoming1)
    sums_out, sums_in = (sums_out0, sums_out1), (sums_in0, sums_in1)

    plane = [
        device_at(add_mod(x, i, 4), add_mod(y, j, 4), z, core) for i in range(4) for j in range(4) if i + j
    ]
    line = [
        device_at(x, y, add_mod(z, i, 4), add_mod(core, j, 2)) for i in range(4) for j in range(2) if i + j
    ]
    barrier = pltpu.get_barrier_semaphore()

    def tell(semaphore, devices):
        for device in devices:
            pl.semaphore_signal(semaphore, inc=1, device_id=device, device_id_type=MESH)

    tell(barrier, plane + line)

    def prepare(u, what):
        if what == "in":
            for at, source in enumerate((in_gain, in_bias)):
                columns[u, at] = jnp.broadcast_to(source[u : u + 1, :], (128, 128)).T
            for part in range(4):
                block = w_in[u, :, part * 128 : (part + 1) * 128].astype(F32).T.astype(BF16)
                for group in range(8):
                    weights[u, group, part * 16 : (part + 1) * 16, :] = block[group * 16 : (group + 1) * 16]
        else:
            gate_t[u] = w_gate[u].astype(F32).T.astype(BF16)
            out_t[u] = w_out[u].astype(F32).T.astype(BF16)
            for at, source in enumerate((mid_gain, mid_bias)):
                columns[u, 2 + at] = jnp.broadcast_to(source[u : u + 1, :], (128, 128)).T

    for load in parameters[:3]:
        load.wait()
    prepare(0, "in")

    def token_rows(tile, quarter):
        start = lax.div(tile, 12) * 1536 + lax.rem(tile, 12) + quarter * 12
        return pl.ds(start, 32, stride=48)

    def enter(pair_of, carry):
        halves = []
        for half in range(2):
            tile = pair_of * 2 + half
            tokens = jnp.concatenate([rows[token_rows(tile, q), :] for q in range(4)], axis=0)
            values = tokens.T
            state[tile] = values
            halves.append(norm_columns(values, columns[0, 0], columns[0, 1]))
        normed[pair_of] = jnp.concatenate(halves, axis=1)
        return carry

    loads[0].wait()
    lax.fori_loop(0, 6, enter, 0, unroll=2)
    pl.semaphore_wait(barrier, len(plane) + len(line))
    tell(plane_sem, line)
    loads[1].wait()
    lax.fori_loop(6, 8, enter, 0, unroll=2)

    others = pl.ds(0, DEVICES - 1)
    slab_left[96:128, :] = jnp.zeros((32, 768), F32)
    slab_right[96:128, :] = jnp.zeros((32, 768), F32)

    def project_and_send(u, part):
        base, count = FIRST_ROW[part], ROWS[part]

        def group_step(group, carry):
            to_y, to_z = add_mod(y_lo, group, 2), add_mod(z_lo, lax.div(group, 2), 2)
            to_core = add_mod(core, lax.div(group, 4), 2)
            which = to_y + to_z * 2 + to_core * 4

            def project(pair_of, inner):
                projected = jnp.dot(weights[u, which], normed[pair_of], preferred_element_type=F32)
                for side in range(2):
                    at = side * 32
                    acts = sigmoid(projected[at : at + 16]) * projected[at + 16 : at + 32]
                    for octet in range(2):
                        for half in range(2):
                            start = octet * 8 * STRIDE + side * count + pair_of * 2 + half - base
                            staged[pl.ds(start, 8, stride=STRIDE), :] = acts[
                                octet * 8 : octet * 8 + 8, half * 128 : half * 128 + 128
                            ]
                return inner

            lax.fori_loop(base // 2, (base + count) // 2, project, 0, unroll=count // 4)

            if u == 0 and part == 0:
                @pl.when(group == 0)
                def _():
                    pl.semaphore_wait(plane_sem, len(line))

            def send(member, inner):
                along = lax.rem(lax.div(member, 4) + lax.rem(member, 4) + 1, 4)
                at_x = add_mod(x, along + core * (4 - 2 * along), 4)
                at_y, at_z = add_mod(y_hi, member, 2), add_mod(z_hi, lax.div(member, 2), 2)
                place = at_x + at_y * 4 + at_z * 8
                channel = which * 16 + place
                outgoing[part][channel] = staged[pl.ds(place * STRIDE, 2 * count), :].astype(BF16)

                @pl.when(channel != my_channel)
                def _():
                    pltpu.make_async_remote_copy(
                        src_ref=outgoing[part].at[channel], dst_ref=incoming[part].at[me],
                        send_sem=send_sem.at[2 * u + part],
                        recv_sem=recv_sem.at[(2 * u + part) * 8 + group],
                        device_id=(at_z * 4 + at_x, at_y * 8 + to_y * 4 + to_z * 2 + to_core),
                        device_id_type=MESH,
                    ).start()

                @pl.when(channel == my_channel)
                def _():
                    pltpu.make_async_copy(
                        outgoing[part].at[channel], incoming[part].at[me], own_sem.at[2 * u + part]
                    ).start()

                return inner

            lax.fori_loop(0, 16, send, 0, unroll=4)
            return carry

        lax.fori_loop(0, 8, group_step, 0)

    project_and_send(0, 0)
    loads[2].wait()
    lax.fori_loop(8, 18, enter, 0, unroll=2)
    project_and_send(0, 1)

    for u in range(2):
        if u == 0:
            for load in parameters[3:]:
                load.wait()
            prepare(0, "out")
            prepare(1, "in")
            prepare(1, "out")

        def gates(pair_of, carry):
            value = sigmoid(jnp.dot(gate_t[u], normed[pair_of], preferred_element_type=F32))
            gate[pair_of * 2] = value[:, :128]
            gate[pair_of * 2 + 1] = value[:, 128:]
            return carry

        lax.fori_loop(0, 18, gates, 0, unroll=2)

        for part in range(2):
            pltpu.make_async_copy(outgoing[part].at[0], incoming[part].at[0], own_sem.at[2 * u + part]).wait()

        def gather(group, carry):
            for part in range(2):
                arrival = recv_sem.at[(2 * u + part) * 8 + group]

                @pl.when(group == 0)
                def _():
                    blocks = incoming[part].at[pl.ds(0, 15)]
                    pltpu.make_async_copy(blocks, blocks, arrival).wait()

                @pl.when(group > 0)
                def _():
                    blocks = incoming[part].at[pl.ds(0, 16)]
                    pltpu.make_async_copy(blocks, blocks, arrival).wait()

            from_y, from_z = add_mod(y_lo, group, 2), add_mod(z_lo, lax.div(group, 2), 2)
            from_core = add_mod(core, lax.div(group, 4), 2)
            column = from_y * 4 + from_z * 2 + from_core
            for h in range(2):
                for hi in range(2):
                    for part in range(2):
                        turned = turn(
                            [incoming[part][(hi * 4 + at) * 16 + h * 8 + column].astype(F32) for at in range(4)]
                        )
                        for quarter in range(4):
                            for at, third, first, count in SEGMENTS[part]:
                                lanes = pl.ds((hi * 3 + third) * 128, 128)
                                to = pl.ds(h * 48 + quarter * 12 + first, count)
                                slab_left[to, lanes] = turned[quarter][at : at + count]
                                at += ROWS[part]
                                slab_right[to, lanes] = turned[quarter][at : at + count]
            if u == 0:
                left16[group] = slab_left[...].astype(BF16)
                for hi in range(2):
                    for third in range(3):
                        lanes = pl.ds((hi * 3 + third) * 128, 128)
                        flipped = slab_right[:, lanes].T.astype(BF16)
                        for at in range(4):
                            right_t[
                                pl.ds((hi * 4 + at) * 96 + third * 32, 32),
                                pl.ds(pl.multiple_of(group * 128, 128), 128),
                            ] = flipped[at * 32 : at * 32 + 32]
            else:
                for h in range(2):
                    right16[h * 8 + column] = slab_right[h * 48 : h * 48 + 48, :].astype(BF16)
                    for part in range(3):
                        sixth = from_core * 3 + part
                        to = h * 384 + lax.div(sixth, 2) * 128 + (from_y * 2 + from_z) * 32 + lax.rem(sixth, 2) * 16
                        at = h * 48 + part * 16
                        left16.reshape(1024, 768)[pl.ds(pl.multiple_of(to, 16), 16), :] = slab_left[
                            at : at + 16, :
                        ].astype(BF16)
            return carry

        lax.fori_loop(0, 8, gather, 0)

        if u == 1:
            for part in range(2):
                pltpu.make_async_copy(
                    sums_out[part].at[others], sums_out[part].at[others], sums_send_sem.at[part]
                ).wait()

        def columns_of(step):
            turn_y = lax.div(step, 2)
            to_y = add_mod(y, turn_y + 1 - 2 * lax.rem(turn_y, 2) + 2 * core, 4)
            return to_y * 2 + add_mod(z_lo, step, 2)

        def multiply(step, summed):
            rows_at = pl.ds(pl.multiple_of(columns_of(step) * 96, 96), 96)
            if u == 0:
                summed[...] = jnp.dot(
                    right_t[rows_at, :], left16.reshape(1024, 768)[...], preferred_element_type=F32
                )
            else:
                summed[...] = lax.dot_general(
                    right16.reshape(768, 768)[rows_at, :], left16.reshape(1024, 768)[0:768, :],
                    (((1,), (1,)), ((), ())), preferred_element_type=F32,
                )

        def send_back(step, part):
            pair_at = columns_of(step)

            def one(index, carry):
                s, to_row = pair_at * 2 + lax.div(index, 8), lax.rem(index, 8)
                to = to_row * 16 + s

                @pl.when(to != me)
                def _():
                    pltpu.make_async_remote_copy(
                        src_ref=sums_out[part].at[to], dst_ref=sums_in[part].at[my_channel],
                        send_sem=sums_send_sem.at[2 * u + part], recv_sem=sums_sem.at[2 * u + part],
                        device_id=(to_row, s), device_id_type=MESH,
                    ).start()

                @pl.when(to == me)
                def _():
                    pltpu.make_async_copy(
                        sums_out[part].at[to], sums_in[part].at[my_channel], own_sums_sem.at[2 * u + part]
                    ).start()

                return carry

            lax.fori_loop(0, 16, one, 0, unroll=4)

        def give_back(steps, carry):
            for parity, (summed, following) in enumerate(((summed0, summed1), (summed1, summed0))):
                step = steps * 2 + parity
                for to_core in range(2):
                    s = columns_of(step) * 2 + to_core
                    for hi in range(2):
                        for quarter in range(4):
                            for third in range(3):
                                piece[to_core * 2 + hi, quarter, third * 12 : third * 12 + 12, :] = summed[
                                    pl.ds(to_core * 48 + quarter * 12, 12), pl.ds((hi * 3 + third) * 128, 128)
                                ]
                for to_core in range(2):
                    s = columns_of(step) * 2 + to_core
                    for hi in range(2):
                        turned = turn([piece[to_core * 2 + hi, quarter] for quarter in range(4)])
                        for at in range(4):
                            to = (hi * 4 + at) * 16 + s
                            sums_out0[to] = turned[at][0:16].astype(BF16)
                            sums_out1[to] = turned[at][16:36].astype(BF16)
                multiply(lax.rem(step + 1, 8), following)
                send_back(step, 0)
            return carry

        multiply(0, summed0)
        lax.fori_loop(0, 4, give_back, 0)

        def give_rest(step, carry):
            send_back(step, 1)
            return carry

        lax.fori_loop(0, 8, give_rest, 0)

        for part in range(2):
            pltpu.make_async_copy(
                outgoing[part].at[others], outgoing[part].at[others], send_sem.at[2 * u + part]
            ).wait()

        def widen(part):
            pltpu.make_async_copy(
                sums_out[part].at[0], sums_in[part].at[0], own_sums_sem.at[2 * u + part]
            ).wait()
            pltpu.make_async_copy(
                sums_in[part].at[others], sums_in[part].at[others], sums_sem.at[2 * u + part]
            ).wait()

            def one(channel, carry):
                to = pl.ds(channel * WIDE + FIRST_ROW[part], ROWS[part])
                widened[to, :] = sums_in[part][channel].astype(F32)
                return carry

            lax.fori_loop(0, DEVICES, one, 0, unroll=8)

        def finish(pair_of, carry):
            mixed = []
            for half in range(2):
                values = widened[pl.ds(pair_of * 2 + half, 128, stride=WIDE), :]
                mixed.append(norm_columns(values, columns[u, 2], columns[u, 3]))
            update = jnp.dot(out_t[u], jnp.concatenate(mixed, axis=1), preferred_element_type=F32)
            halves = []
            for half in range(2):
                tile = pair_of * 2 + half
                values = state[tile] + gate[tile] * update[:, half * 128 : half * 128 + 128]
                if u == 0:
                    state[tile] = values
                    halves.append(norm_columns(values, columns[1, 0], columns[1, 1]))
                else:
                    tokens = values.T
                    for q in range(4):
                        rows[token_rows(tile, q), :] = tokens[q * 32 : q * 32 + 32]
            if u == 0:
                normed[pair_of] = jnp.concatenate(halves, axis=1)
            return carry

        widen(0)
        if u == 0:
            lax.fori_loop(0, 8, finish, 0, unroll=2)
            project_and_send(1, 0)
            widen(1)
            lax.fori_loop(8, 18, finish, 0, unroll=2)
            project_and_send(1, 1)
        else:
            stores = [
                pltpu.make_async_copy(
                    rows.at[pl.ds(i * 1536, 1536)], out.at[pl.ds(i * 1536, 1536)], copy_sem.at[i]
                )
                for i in range(3)
            ]
            lax.fori_loop(0, 6, finish, 0, unroll=2)
            stores[0].start()
            lax.fori_loop(6, 8, finish, 0, unroll=2)
            widen(1)
            lax.fori_loop(8, 12, finish, 0, unroll=2)
            stores[1].start()
            lax.fori_loop(12, 18, finish, 0, unroll=2)
            stores[2].start()

    for part in range(2):
        pltpu.make_async_copy(
            sums_out[part].at[others], sums_out[part].at[others], sums_send_sem.at[2 + part]
        ).wait()
    for store in stores:
        store.wait()


def local(pair, *parameters):
    anywhere = pl.BlockSpec(memory_space=pl.ANY)
    done = pl.pallas_call(
        kernel,
        out_shape=jax.ShapeDtypeStruct((4608, 128), F32),
        in_specs=[anywhere] * 8,
        out_specs=anywhere,
        scratch_shapes=[pltpu.VMEM(p.shape, p.dtype) for p in parameters] + [
            pltpu.VMEM((4608, 128), F32),
            pltpu.VMEM((36, 128, 128), F32),
            pltpu.VMEM((36, 128, 128), F32),
            pltpu.VMEM((18, 128, 256), BF16),
            pltpu.VMEM((16 * STRIDE + 8, 128), F32),
            pltpu.VMEM((128 * WIDE, 128), F32),
            pltpu.VMEM((128, 32, 128), BF16),
            pltpu.VMEM((128, 40, 128), BF16),
            pltpu.VMEM((128, 32, 128), BF16),
            pltpu.VMEM((128, 40, 128), BF16),
            pltpu.VMEM((128, 16, 128), BF16),
            pltpu.VMEM((128, 20, 128), BF16),
            pltpu.VMEM((128, 16, 128), BF16),
            pltpu.VMEM((128, 20, 128), BF16),
            pltpu.VMEM((128, 768), F32),
            pltpu.VMEM((128, 768), F32),
            pltpu.VMEM((8, 128, 768), BF16),
            pltpu.VMEM((16, 48, 768), BF16),
            pltpu.VMEM((768, 1024), BF16),
            pltpu.VMEM((96, 768), F32),
            pltpu.VMEM((96, 768), F32),
            pltpu.VMEM((4, 4, 36, 128), F32),
            pltpu.VMEM((2, 8, 64, 128), BF16),
            pltpu.VMEM((2, 128, 128), BF16),
            pltpu.VMEM((2, 128, 128), BF16),
            pltpu.VMEM((2, 4, 128, 128), F32),
            pltpu.SemaphoreType.DMA((3,)),
            pltpu.SemaphoreType.DMA((7,)),
            pltpu.SemaphoreType.DMA((4,)),
            pltpu.SemaphoreType.DMA((4,)),
            pltpu.SemaphoreType.DMA((4,)),
            pltpu.SemaphoreType.DMA((4,)),
            pltpu.SemaphoreType.DMA((32,)),
            pltpu.SemaphoreType.DMA((4,)),
            pltpu.SemaphoreType.REGULAR,
        ],
        compiler_params=pltpu.CompilerParams(
            collective_id=0, has_side_effects=True, vmem_limit_bytes=56 * 2**20
        ),
    )(pair.reshape(4608, 128), *parameters)
    return done.reshape(96, 48, 128)


def solution(mesh):
    return jax.shard_map(
        local,
        mesh=mesh,
        in_specs=(P("row", "col", None), P(), P(), P(), P(), P(), P(), P()),
        out_specs=P("row", "col", None),
        check_vma=False,
    )
```

```python
import jax
import jax.numpy as jnp
from jax import lax
from jax.experimental import pallas as pl
from jax.experimental.pallas import tpu as pltpu
from jax.sharding import PartitionSpec as P

epsilon = 1e-05
MESH = pl.DeviceIdType.MESH
DEVICES = 128
F32, BF16 = jnp.float32, jnp.bfloat16
STRIDE = 41
WIDE = 41
FIRST_ROW, ROWS = (0, 16), (16, 20)
RANGES = (((0, 8, 0, 16),), ((8, 12, 0, 8), (12, 18, 16, 12)))
SEGMENTS = (
    ((0, 16, 0, 0, 8), (8, 24, 1, 0, 8)),
    ((0, 8, 2, 0, 8), (16, 28, 0, 8, 4), (20, 32, 1, 8, 4), (24, 36, 2, 8, 4)),
)


def add_mod(value, offset, size):
    return lax.rem(value + offset, size)


def device_at(x, y, z, core):
    return lax.div(z, 2) * 4 + x, y * 4 + lax.rem(z, 2) * 2 + core


def sigmoid(values):
    return 0.5 * jnp.tanh(0.5 * values) + 0.5


def norm_columns(values, gain, bias):
    centre = jnp.mean(values, axis=0, keepdims=True)
    shifted = values - centre
    spread = jnp.mean(shifted * shifted, axis=0, keepdims=True)
    return (shifted * lax.rsqrt(spread + epsilon) * gain + bias).astype(BF16)


def turn(blocks):
    lane = lax.broadcasted_iota(jnp.int32, blocks[0].shape, 1)
    first, even = lane < 64, lane % 64 < 32
    a0, a1, a2, a3 = blocks
    b0, b2 = jnp.where(first, a0, pltpu.roll(a2, 64, 1)), jnp.where(first, pltpu.roll(a0, 64, 1), a2)
    b1, b3 = jnp.where(first, a1, pltpu.roll(a3, 64, 1)), jnp.where(first, pltpu.roll(a1, 64, 1), a3)
    c0, c1 = jnp.where(even, b0, pltpu.roll(b1, 32, 1)), jnp.where(even, pltpu.roll(b0, 96, 1), b1)
    c2, c3 = jnp.where(even, b2, pltpu.roll(b3, 32, 1)), jnp.where(even, pltpu.roll(b2, 96, 1), b3)
    return c0, c1, c2, c3


def kernel(
    pair, in_gain_h, in_bias_h, mid_gain_h, mid_bias_h, w_in_h, w_gate_h, w_out_h, out,
    in_gain, in_bias, mid_gain, mid_bias, w_in, w_gate, w_out,
    rows, state, gate, normed, staged, widened, outgoing0, outgoing1, incoming0, incoming1,
    sums_out0, sums_out1, sums_in0, sums_in1,
    slab_left, slab_right, flipped_rows, compact, left16, right16, right_t, summed0, summed1, weights, gate_t, out_t, columns,
    copy_sem, param_sem, own_sem, own_sums_sem, send_sem, sums_send_sem, recv_sem, sums_sem, plane_sem,
):
    row, col = lax.axis_index("row"), lax.axis_index("col")
    me = row * 16 + col
    x, z_hi = lax.rem(row, 4), lax.div(row, 4)
    y, z_lo, core = lax.div(col, 4), lax.rem(lax.div(col, 2), 2), lax.rem(col, 2)
    z = z_hi * 2 + z_lo
    y_lo, y_hi = lax.rem(y, 2), lax.div(y, 2)
    my_channel = (y_lo + z_lo * 2 + core * 4) * 16 + x + y_hi * 4 + z_hi * 8

    loads = [
        pltpu.make_async_copy(pair.at[pl.ds(i * 1536, 1536)], rows.at[pl.ds(i * 1536, 1536)], copy_sem.at[i])
        for i in range(3)
    ]
    parameters = [
        pltpu.make_async_copy(from_hbm, to, param_sem.at[i])
        for i, (from_hbm, to) in enumerate(
            (
                (in_gain_h, in_gain), (in_bias_h, in_bias), (w_in_h, w_in), (mid_gain_h, mid_gain),
                (mid_bias_h, mid_bias), (w_gate_h, w_gate), (w_out_h, w_out),
            )
        )
    ]
    for load in parameters[:3] + loads + parameters[3:]:
        load.start()

    outgoing, incoming = (outgoing0, outgoing1), (incoming0, incoming1)
    sums_out, sums_in = (sums_out0, sums_out1), (sums_in0, sums_in1)

    on_x, on_y, on_z = ([add_mod(at, i, 4) for i in range(4)] for at in (x, y, z))
    same_core = [
        device_at(on_x[i], on_y[j], on_z[k], core)
        for i in (2, 1, 3, 0) for j in (2, 1, 3, 0) for k in (2, 1, 3, 0) if i + j + k
    ]
    other_core = [device_at(x, y, z, 1 - core)]
    barrier = pltpu.get_barrier_semaphore()

    def tell(semaphore, devices):
        for device in devices:
            pl.semaphore_signal(semaphore, inc=1, device_id=device, device_id_type=MESH)

    tell(barrier, same_core + other_core)

    def prepare(u, what):
        if what == "in":
            for at, source in enumerate((in_gain, in_bias)):
                columns[u, at] = jnp.broadcast_to(source[u : u + 1, :], (128, 128)).T
            for part in range(4):
                block = w_in[u, :, part * 128 : (part + 1) * 128].astype(F32).T.astype(BF16)
                for group in range(8):
                    weights[u, group, part * 16 : (part + 1) * 16, :] = block[group * 16 : (group + 1) * 16]
        else:
            gate_t[u] = w_gate[u].astype(F32).T.astype(BF16)
            out_t[u] = w_out[u].astype(F32).T.astype(BF16)
            for at, source in enumerate((mid_gain, mid_bias)):
                columns[u, 2 + at] = jnp.broadcast_to(source[u : u + 1, :], (128, 128)).T

    for load in parameters[:3]:
        load.wait()
    prepare(0, "in")

    def token_rows(tile, quarter):
        late = lax.div(tile, 24)
        third = (1 - late) * lax.div(tile, 8) + late * lax.div(tile - 24 * late, 4)
        b0 = (1 - late) * lax.rem(tile, 8) + late * (8 + lax.rem(tile, 4))
        start = third * 1536 + b0 + quarter * 12
        return pl.ds(start, 32, stride=48)

    def enter(pair_of, carry):
        halves = []
        for half in range(2):
            tile = pair_of * 2 + half
            tokens = jnp.concatenate([rows[token_rows(tile, q), :] for q in range(4)], axis=0)
            values = tokens.T
            state[tile] = values
            halves.append(norm_columns(values, columns[0, 0], columns[0, 1]))
        normed[pair_of] = jnp.concatenate(halves, axis=1)
        return carry

    loads[0].wait()
    lax.fori_loop(0, 4, enter, 0, unroll=2)
    pl.semaphore_wait(barrier, 64)
    tell(plane_sem, other_core)
    loads[1].wait()
    lax.fori_loop(4, 8, enter, 0, unroll=2)

    others = pl.ds(0, DEVICES - 1)
    slab_left[...] = jnp.zeros((128, 768), F32)
    slab_right[...] = jnp.zeros((128, 768), F32)
    flipped_rows[...] = jnp.zeros((1024, 128), F32)

    def project_and_send(u, part):
        count = ROWS[part]

        def group_step(group, carry):
            to_y, to_z = add_mod(y_lo, group, 2), add_mod(z_lo, lax.div(group, 2), 2)
            to_core = add_mod(core, lax.div(group, 4), 2)
            which = to_y + to_z * 2 + to_core * 4

            for first, last, row_at, side_step in RANGES[part]:

                def project(pair_of, inner):
                    projected = jnp.dot(weights[u, which], normed[pair_of], preferred_element_type=F32)
                    for side in range(2):
                        at = side * 32
                        acts = sigmoid(projected[at : at + 16]) * projected[at + 16 : at + 32]
                        for octet in range(2):
                            for half in range(2):
                                to = row_at + side * side_step + (pair_of - first) * 2 + half
                                staged[pl.ds(octet * 8 * STRIDE + to, 8, stride=STRIDE), :] = acts[
                                    octet * 8 : octet * 8 + 8, half * 128 : half * 128 + 128
                                ]
                    return inner

                lax.fori_loop(first, last, project, 0, unroll=3 if last - first == 6 else 4)

            if u == 0 and part == 0:
                @pl.when(group == 0)
                def _():
                    pl.semaphore_wait(plane_sem, 1)

            def send(member, inner):
                along = lax.rem(lax.div(member, 4) + lax.rem(member, 4), 4)
                at_x = add_mod(x, along + core * (4 - 2 * along), 4)
                at_y, at_z = add_mod(y_hi, member, 2), add_mod(z_hi, lax.div(member, 2), 2)
                place = at_x + at_y * 4 + at_z * 8
                channel = which * 16 + place
                outgoing[part][channel] = staged[pl.ds(place * STRIDE, 2 * count), :].astype(BF16)

                def remote():
                    pltpu.make_async_remote_copy(
                        src_ref=outgoing[part].at[channel], dst_ref=incoming[part].at[me],
                        send_sem=send_sem.at[2 * u + part],
                        recv_sem=recv_sem.at[(2 * u + part) * 8 + group],
                        device_id=(at_z * 4 + at_x, at_y * 8 + to_y * 4 + to_z * 2 + to_core),
                        device_id_type=MESH,
                    ).start()

                if isinstance(member, int):
                    pl.when(group > 0)(remote)

                    @pl.when(group == 0)
                    def _():
                        pltpu.make_async_copy(
                            outgoing[part].at[channel], incoming[part].at[me], own_sem.at[2 * u + part]
                        ).start()
                else:
                    remote()
                return inner

            send(0, 0)
            lax.fori_loop(1, 16, send, 0, unroll=15)
            return carry

        lax.fori_loop(0, 8, group_step, 0)

    project_and_send(0, 0)
    loads[2].wait()
    lax.fori_loop(8, 18, enter, 0, unroll=2)
    project_and_send(0, 1)

    for u in range(2):
        if u == 0:
            for load in parameters[3:]:
                load.wait()
            prepare(0, "out")
            prepare(1, "in")
            prepare(1, "out")

        def gates(pair_of, carry):
            value = sigmoid(jnp.dot(gate_t[u], normed[pair_of], preferred_element_type=F32))
            gate[pair_of * 2] = value[:, :128]
            gate[pair_of * 2 + 1] = value[:, 128:]
            return carry

        lax.fori_loop(0, 18, gates, 0, unroll=2)

        for part in range(2):
            pltpu.make_async_copy(outgoing[part].at[0], incoming[part].at[0], own_sem.at[2 * u + part]).wait()

        def gather(group, carry):
            for part in range(2):
                arrival = recv_sem.at[(2 * u + part) * 8 + group]

                @pl.when(group == 0)
                def _():
                    blocks = incoming[part].at[pl.ds(0, 15)]
                    pltpu.make_async_copy(blocks, blocks, arrival).wait()

                @pl.when(group > 0)
                def _():
                    blocks = incoming[part].at[pl.ds(0, 16)]
                    pltpu.make_async_copy(blocks, blocks, arrival).wait()

            from_y, from_z = add_mod(y_lo, group, 2), add_mod(z_lo, lax.div(group, 2), 2)
            from_core = add_mod(core, lax.div(group, 4), 2)
            column = from_y * 4 + from_z * 2 + from_core
            for h in range(2):
                for hi in range(2):
                    for part in range(2):
                        turned = turn(
                            [incoming[part][(hi * 4 + at) * 16 + h * 8 + column].astype(F32) for at in range(4)]
                        )
                        for quarter in range(4):
                            for left_at, right_at, third, first, count in SEGMENTS[part]:
                                lanes = pl.ds((hi * 3 + third) * 128, 128)
                                to = pl.ds(h * 64 + quarter * 16 + first, count)
                                slab_left[to, lanes] = turned[quarter][left_at : left_at + count]
                                slab_right[to, lanes] = turned[quarter][right_at : right_at + count]
            if u == 0:
                left16[group] = slab_left[...].astype(BF16)
                for hi in range(2):
                    for third in range(3):
                        lanes = pl.ds((hi * 3 + third) * 128, 128)
                        flipped = slab_right[:, lanes].T
                        for at in range(4):
                            now, end = third * 32, third * 32 + 32
                            while now < end:
                                twelfth, within = now // 12, now % 12
                                count = min(12 - within, end - now)
                                to = (hi * 4 + at) * 128 + twelfth * 16 + within
                                source = at * 32 + now - third * 32
                                flipped_rows[to : to + count, :] = flipped[source : source + count]
                                now += count
                right_t[:, pl.ds(pl.multiple_of(group * 128, 128), 128)] = flipped_rows[...].astype(BF16)
            else:
                for h in range(2):
                    right16[h * 8 + column] = slab_right[h * 64 : h * 64 + 64, :].astype(BF16)
                    for quarter in range(4):
                        at = h * 64 + quarter * 16
                        compact[h, quarter * 12 : quarter * 12 + 12, :] = slab_left[at : at + 12, :]
                    for part in range(3):
                        sixth = from_core * 3 + part
                        to = h * 384 + lax.div(sixth, 2) * 128 + (from_y * 2 + from_z) * 32 + lax.rem(sixth, 2) * 16
                        left16.reshape(1024, 768)[pl.ds(pl.multiple_of(to, 16), 16), :] = compact[
                            h, part * 16 : part * 16 + 16, :
                        ].astype(BF16)
            return carry

        lax.fori_loop(0, 8, gather, 0)

        if u == 1:
            for part in range(2):
                pltpu.make_async_copy(
                    sums_out[part].at[others], sums_out[part].at[others], sums_send_sem.at[part]
                ).wait()

        def columns_of(step):
            turn_y = lax.div(step, 2)
            late = lax.div(turn_y, 2)
            to_y = add_mod(y, (1 - late) * (2 - 2 * turn_y) + late * (2 * turn_y - 3) + 2 * core, 4)
            return to_y * 2 + add_mod(z_lo, step, 2)

        def multiply(step, summed):
            rows_at = pl.ds(pl.multiple_of(columns_of(step) * 128, 128), 128)
            if u == 0:
                summed[...] = jnp.dot(
                    right_t[rows_at, :], left16.reshape(1024, 768)[...], preferred_element_type=F32
                )
            else:
                summed[...] = lax.dot_general(
                    right16.reshape(1024, 768)[rows_at, :], left16.reshape(1024, 768)[0:768, :],
                    (((1,), (1,)), ((), ())), preferred_element_type=F32,
                )

        def send_back(step, part):
            pair_at = columns_of(step)

            def one(member, carry):
                to_x = add_mod(x, lax.div(member, 4) + lax.rem(member, 4), 4)
                to_row = add_mod(z_hi, member, 2) * 4 + to_x
                s = pair_at * 2 + add_mod(core, lax.div(member, 2), 2)
                to = to_row * 16 + s

                def remote():
                    pltpu.make_async_remote_copy(
                        src_ref=sums_out[part].at[to], dst_ref=sums_in[part].at[my_channel],
                        send_sem=sums_send_sem.at[2 * u + part], recv_sem=sums_sem.at[2 * u + part],
                        device_id=(to_row, s), device_id_type=MESH,
                    ).start()

                if isinstance(member, int):
                    pl.when(to != me)(remote)

                    @pl.when(to == me)
                    def _():
                        pltpu.make_async_copy(
                            sums_out[part].at[to], sums_in[part].at[my_channel], own_sums_sem.at[2 * u + part]
                        ).start()
                else:
                    remote()
                return carry

            one(0, 0)
            lax.fori_loop(1, 16, one, 0, unroll=15)

        def give_back(steps, carry):
            for parity, (summed, following) in enumerate(((summed0, summed1), (summed1, summed0))):
                step = steps * 2 + parity
                for to_core in range(2):
                    s = columns_of(step) * 2 + to_core
                    for hi in range(2):
                        for part in range(2):
                            blocks = []
                            for quarter in range(4):
                                at = to_core * 64 + quarter * 16
                                pieces = [
                                    summed[pl.ds(at + first, count), pl.ds((hi * 3 + third) * 128, 128)]
                                    for _, _, third, first, count in SEGMENTS[part]
                                ]
                                blocks.append(jnp.concatenate(pieces, axis=0))
                            turned = turn(blocks)
                            for at in range(4):
                                to = (hi * 4 + at) * 16 + s
                                if part == 0:
                                    sums_out0[to] = turned[at].astype(BF16)
                                else:
                                    for four in range(5):
                                        sums_out1[to, four] = turned[at][four * 4 : four * 4 + 4].astype(BF16)
                multiply(lax.rem(step + 1, 8), following)
                send_back(step, 0)
            return carry

        multiply(0, summed0)
        lax.fori_loop(0, 4, give_back, 0)

        def give_rest(step, carry):
            send_back(step, 1)
            return carry

        lax.fori_loop(0, 8, give_rest, 0)

        for part in range(2):
            pltpu.make_async_copy(
                outgoing[part].at[others], outgoing[part].at[others], send_sem.at[2 * u + part]
            ).wait()

        def widen(part):
            pltpu.make_async_copy(
                sums_out[part].at[0], sums_in[part].at[0], own_sums_sem.at[2 * u + part]
            ).wait()
            pltpu.make_async_copy(
                sums_in[part].at[others], sums_in[part].at[others], sums_sem.at[2 * u + part]
            ).wait()

            def one(channel, carry):
                to = channel * WIDE + FIRST_ROW[part]
                if part == 0:
                    widened[pl.ds(to, 16), :] = sums_in0[channel].astype(F32)
                else:
                    for four in range(5):
                        widened[pl.ds(to + four * 4, 4), :] = sums_in1[channel, four].astype(F32)
                return carry

            lax.fori_loop(0, DEVICES, one, 0, unroll=8)

        def finish(pair_of, carry):
            mixed = []
            for half in range(2):
                values = widened[pl.ds(pair_of * 2 + half, 128, stride=WIDE), :]
                mixed.append(norm_columns(values, columns[u, 2], columns[u, 3]))
            update = jnp.dot(out_t[u], jnp.concatenate(mixed, axis=1), preferred_element_type=F32)
            halves = []
            for half in range(2):
                tile = pair_of * 2 + half
                values = state[tile] + gate[tile] * update[:, half * 128 : half * 128 + 128]
                if u == 0:
                    state[tile] = values
                    halves.append(norm_columns(values, columns[1, 0], columns[1, 1]))
                else:
                    tokens = values.T
                    for q in range(4):
                        rows[token_rows(tile, q), :] = tokens[q * 32 : q * 32 + 32]
            if u == 0:
                normed[pair_of] = jnp.concatenate(halves, axis=1)
            return carry

        widen(0)
        if u == 0:
            lax.fori_loop(0, 8, finish, 0, unroll=2)
            project_and_send(1, 0)
            widen(1)
            lax.fori_loop(8, 18, finish, 0, unroll=2)
            project_and_send(1, 1)
        else:
            stores = [
                pltpu.make_async_copy(
                    rows.at[pl.ds(i * 1536, 1536)], out.at[pl.ds(i * 1536, 1536)], copy_sem.at[i]
                )
                for i in range(3)
            ]
            lax.fori_loop(0, 8, finish, 0, unroll=2)
            widen(1)
            lax.fori_loop(8, 14, finish, 0, unroll=2)
            stores[0].start()
            lax.fori_loop(14, 16, finish, 0, unroll=2)
            stores[1].start()
            lax.fori_loop(16, 18, finish, 0, unroll=2)
            stores[2].start()

    for part in range(2):
        pltpu.make_async_copy(
            sums_out[part].at[others], sums_out[part].at[others], sums_send_sem.at[2 + part]
        ).wait()
    for store in stores:
        store.wait()


def local(pair, *parameters):
    anywhere = pl.BlockSpec(memory_space=pl.ANY)
    done = pl.pallas_call(
        kernel,
        out_shape=jax.ShapeDtypeStruct((4608, 128), F32),
        in_specs=[anywhere] * 8,
        out_specs=anywhere,
        scratch_shapes=[pltpu.VMEM(p.shape, p.dtype) for p in parameters] + [
            pltpu.VMEM((4608, 128), F32),
            pltpu.VMEM((36, 128, 128), F32),
            pltpu.VMEM((36, 128, 128), F32),
            pltpu.VMEM((18, 128, 256), BF16),
            pltpu.VMEM((16 * STRIDE + 8, 128), F32),
            pltpu.VMEM((128 * WIDE, 128), F32),
            pltpu.VMEM((128, 32, 128), BF16),
            pltpu.VMEM((128, 40, 128), BF16),
            pltpu.VMEM((128, 32, 128), BF16),
            pltpu.VMEM((128, 40, 128), BF16),
            pltpu.VMEM((128, 16, 128), BF16),
            pltpu.VMEM((128, 5, 4, 128), BF16),
            pltpu.VMEM((128, 16, 128), BF16),
            pltpu.VMEM((128, 5, 4, 128), BF16),
            pltpu.VMEM((128, 768), F32),
            pltpu.VMEM((128, 768), F32),
            pltpu.VMEM((1024, 128), F32),
            pltpu.VMEM((2, 48, 768), F32),
            pltpu.VMEM((8, 128, 768), BF16),
            pltpu.VMEM((16, 64, 768), BF16),
            pltpu.VMEM((1024, 1024), BF16),
            pltpu.VMEM((128, 768), F32),
            pltpu.VMEM((128, 768), F32),
            pltpu.VMEM((2, 8, 64, 128), BF16),
            pltpu.VMEM((2, 128, 128), BF16),
            pltpu.VMEM((2, 128, 128), BF16),
            pltpu.VMEM((2, 4, 128, 128), F32),
            pltpu.SemaphoreType.DMA((3,)),
            pltpu.SemaphoreType.DMA((7,)),
            pltpu.SemaphoreType.DMA((4,)),
            pltpu.SemaphoreType.DMA((4,)),
            pltpu.SemaphoreType.DMA((4,)),
            pltpu.SemaphoreType.DMA((4,)),
            pltpu.SemaphoreType.DMA((32,)),
            pltpu.SemaphoreType.DMA((4,)),
            pltpu.SemaphoreType.REGULAR,
        ],
        compiler_params=pltpu.CompilerParams(
            collective_id=0, has_side_effects=True, vmem_limit_bytes=56 * 2**20
        ),
    )(pair.reshape(4608, 128), *parameters)
    return done.reshape(96, 48, 128)


def solution(mesh):
    return jax.shard_map(
        local,
        mesh=mesh,
        in_specs=(P("row", "col", None), P(), P(), P(), P(), P(), P(), P()),
        out_specs=P("row", "col", None),
        check_vma=False,
    )
```

```python
import jax
import jax.numpy as jnp
from jax import lax
from jax.experimental import pallas as pl
from jax.experimental.pallas import tpu as pltpu
from jax.sharding import PartitionSpec as P

epsilon = 1e-05
MESH = pl.DeviceIdType.MESH
DEVICES = 128
F32, BF16 = jnp.float32, jnp.bfloat16
STRIDE = 41
WIDE = 41
FIRST_ROW, ROWS = (0, 16), (16, 20)
RANGES = (((0, 8, 0, 16),), ((8, 12, 0, 8), (12, 18, 16, 12)))
SEGMENTS = (
    ((0, 16, 0, 0, 8), (8, 24, 1, 0, 8)),
    ((0, 8, 2, 0, 8), (16, 28, 0, 8, 4), (20, 32, 1, 8, 4), (24, 36, 2, 8, 4)),
)


def add_mod(value, offset, size):
    return lax.rem(value + offset, size)


def device_at(x, y, z, core):
    return lax.div(z, 2) * 4 + x, y * 4 + lax.rem(z, 2) * 2 + core


def offset_along(member, ending):
    quad = lax.div(member, 4)
    late = lax.div(quad, 2)
    far = (1 - late) * (2 - quad) + late * (9 - 3 * quad)
    return (1 - ending) * lax.rem(quad + lax.rem(member, 4), 4) + ending * far


def sigmoid(values):
    return 0.5 * jnp.tanh(0.5 * values) + 0.5


def norm_columns(values, gain, bias):
    centre = jnp.mean(values, axis=0, keepdims=True)
    shifted = values - centre
    spread = jnp.mean(shifted * shifted, axis=0, keepdims=True)
    return (shifted * lax.rsqrt(spread + epsilon) * gain + bias).astype(BF16)


def turn(blocks):
    lane = lax.broadcasted_iota(jnp.int32, blocks[0].shape, 1)
    first, even = lane < 64, lane % 64 < 32
    a0, a1, a2, a3 = blocks
    b0, b2 = jnp.where(first, a0, pltpu.roll(a2, 64, 1)), jnp.where(first, pltpu.roll(a0, 64, 1), a2)
    b1, b3 = jnp.where(first, a1, pltpu.roll(a3, 64, 1)), jnp.where(first, pltpu.roll(a1, 64, 1), a3)
    c0, c1 = jnp.where(even, b0, pltpu.roll(b1, 32, 1)), jnp.where(even, pltpu.roll(b0, 96, 1), b1)
    c2, c3 = jnp.where(even, b2, pltpu.roll(b3, 32, 1)), jnp.where(even, pltpu.roll(b2, 96, 1), b3)
    return c0, c1, c2, c3


def kernel(
    pair, in_gain_h, in_bias_h, mid_gain_h, mid_bias_h, w_in_h, w_gate_h, w_out_h, out,
    in_gain, in_bias, mid_gain, mid_bias, w_in, w_gate, w_out,
    rows, state, gate, normed, staged, widened, outgoing0, outgoing1, incoming0, incoming1,
    sums_out0, sums_out1, sums_in0, sums_in1,
    slab_left, slab_right, flipped_rows, compact, left16, right16, right_t, summed0, summed1, weights, gate_t, out_t, columns,
    copy_sem, param_sem, own_sem, own_sums_sem, send_sem, sums_send_sem, recv_sem, sums_sem, plane_sem,
):
    row, col = lax.axis_index("row"), lax.axis_index("col")
    me = row * 16 + col
    x, z_hi = lax.rem(row, 4), lax.div(row, 4)
    y, z_lo, core = lax.div(col, 4), lax.rem(lax.div(col, 2), 2), lax.rem(col, 2)
    z = z_hi * 2 + z_lo
    y_lo, y_hi = lax.rem(y, 2), lax.div(y, 2)
    my_channel = (y_lo + z_lo * 2 + core * 4) * 16 + x + y_hi * 4 + z_hi * 8

    loads = [
        pltpu.make_async_copy(pair.at[pl.ds(i * 1536, 1536)], rows.at[pl.ds(i * 1536, 1536)], copy_sem.at[i])
        for i in range(3)
    ]
    parameters = [
        pltpu.make_async_copy(from_hbm, to, param_sem.at[i])
        for i, (from_hbm, to) in enumerate(
            (
                (in_gain_h, in_gain), (in_bias_h, in_bias), (w_in_h, w_in), (mid_gain_h, mid_gain),
                (mid_bias_h, mid_bias), (w_gate_h, w_gate), (w_out_h, w_out),
            )
        )
    ]
    for load in parameters[:3] + loads + parameters[3:]:
        load.start()

    outgoing, incoming = (outgoing0, outgoing1), (incoming0, incoming1)
    sums_out, sums_in = (sums_out0, sums_out1), (sums_in0, sums_in1)

    on_x, on_y, on_z = ([add_mod(at, i, 4) for i in range(4)] for at in (x, y, z))
    same_core = [
        device_at(on_x[i], on_y[j], on_z[k], core)
        for i in (2, 1, 3, 0) for j in (2, 1, 3, 0) for k in (2, 1, 3, 0) if i + j + k
    ]
    other_core = [device_at(x, y, z, 1 - core)]
    barrier = pltpu.get_barrier_semaphore()

    def tell(semaphore, devices):
        for device in devices:
            pl.semaphore_signal(semaphore, inc=1, device_id=device, device_id_type=MESH)

    tell(barrier, same_core + other_core)

    def prepare(u, what):
        if what == "in":
            for at, source in enumerate((in_gain, in_bias)):
                columns[u, at] = jnp.broadcast_to(source[u : u + 1, :], (128, 128)).T
            for part in range(4):
                block = w_in[u, :, part * 128 : (part + 1) * 128].astype(F32).T.astype(BF16)
                for group in range(8):
                    weights[u, group, part * 16 : (part + 1) * 16, :] = block[group * 16 : (group + 1) * 16]
        else:
            gate_t[u] = w_gate[u].astype(F32).T.astype(BF16)
            out_t[u] = w_out[u].astype(F32).T.astype(BF16)
            for at, source in enumerate((mid_gain, mid_bias)):
                columns[u, 2 + at] = jnp.broadcast_to(source[u : u + 1, :], (128, 128)).T

    for load in parameters[:3]:
        load.wait()
    prepare(0, "in")

    def token_rows(tile, quarter):
        late = lax.div(tile, 24)
        third = (1 - late) * lax.div(tile, 8) + late * lax.div(tile - 24 * late, 4)
        b0 = (1 - late) * lax.rem(tile, 8) + late * (8 + lax.rem(tile, 4))
        start = third * 1536 + b0 + quarter * 12
        return pl.ds(start, 32, stride=48)

    def enter(pair_of, carry):
        halves = []
        for half in range(2):
            tile = pair_of * 2 + half
            tokens = jnp.concatenate([rows[token_rows(tile, q), :] for q in range(4)], axis=0)
            values = tokens.T
            state[tile] = values
            halves.append(norm_columns(values, columns[0, 0], columns[0, 1]))
        normed[pair_of] = jnp.concatenate(halves, axis=1)
        return carry

    loads[0].wait()
    lax.fori_loop(0, 4, enter, 0, unroll=2)
    pl.semaphore_wait(barrier, 64)
    tell(plane_sem, other_core)
    loads[1].wait()
    lax.fori_loop(4, 8, enter, 0, unroll=2)

    others = pl.ds(0, DEVICES - 1)
    slab_left[...] = jnp.zeros((128, 768), F32)
    slab_right[...] = jnp.zeros((128, 768), F32)
    flipped_rows[...] = jnp.zeros((1024, 128), F32)

    def project_and_send(u, part):
        count = ROWS[part]

        def group_step(group, carry):
            to_y, to_z = add_mod(y_lo, group, 2), add_mod(z_lo, lax.div(group, 2), 2)
            to_core = add_mod(core, lax.div(group, 4), 2)
            which = to_y + to_z * 2 + to_core * 4

            for first, last, row_at, side_step in RANGES[part]:

                def project(pair_of, inner):
                    projected = jnp.dot(weights[u, which], normed[pair_of], preferred_element_type=F32)
                    for side in range(2):
                        at = side * 32
                        acts = sigmoid(projected[at : at + 16]) * projected[at + 16 : at + 32]
                        for octet in range(2):
                            for half in range(2):
                                to = row_at + side * side_step + (pair_of - first) * 2 + half
                                staged[pl.ds(octet * 8 * STRIDE + to, 8, stride=STRIDE), :] = acts[
                                    octet * 8 : octet * 8 + 8, half * 128 : half * 128 + 128
                                ]
                    return inner

                lax.fori_loop(first, last, project, 0, unroll=3 if last - first == 6 else 4)

            if u == 0 and part == 0:
                @pl.when(group == 0)
                def _():
                    pl.semaphore_wait(plane_sem, 1)

            def send(member, inner):
                along = offset_along(member, lax.div(group, 7) * part)
                at_x = add_mod(x, along + core * (4 - 2 * along), 4)
                at_y, at_z = add_mod(y_hi, member, 2), add_mod(z_hi, lax.div(member, 2), 2)
                place = at_x + at_y * 4 + at_z * 8
                channel = which * 16 + place
                outgoing[part][channel] = staged[pl.ds(place * STRIDE, 2 * count), :].astype(BF16)

                def remote():
                    pltpu.make_async_remote_copy(
                        src_ref=outgoing[part].at[channel], dst_ref=incoming[part].at[me],
                        send_sem=send_sem.at[2 * u + part],
                        recv_sem=recv_sem.at[(2 * u + part) * 8 + group],
                        device_id=(at_z * 4 + at_x, at_y * 8 + to_y * 4 + to_z * 2 + to_core),
                        device_id_type=MESH,
                    ).start()

                if isinstance(member, int):
                    pl.when(group > 0)(remote)

                    @pl.when(group == 0)
                    def _():
                        pltpu.make_async_copy(
                            outgoing[part].at[channel], incoming[part].at[me], own_sem.at[2 * u + part]
                        ).start()
                else:
                    remote()
                return inner

            send(0, 0)
            lax.fori_loop(1, 16, send, 0, unroll=15)
            return carry

        lax.fori_loop(0, 8, group_step, 0)

    project_and_send(0, 0)
    loads[2].wait()
    lax.fori_loop(8, 18, enter, 0, unroll=2)
    project_and_send(0, 1)

    for u in range(2):
        if u == 0:
            for load in parameters[3:]:
                load.wait()
            prepare(0, "out")
            prepare(1, "in")
            prepare(1, "out")

        def gates(pair_of, carry):
            value = sigmoid(jnp.dot(gate_t[u], normed[pair_of], preferred_element_type=F32))
            gate[pair_of * 2] = value[:, :128]
            gate[pair_of * 2 + 1] = value[:, 128:]
            return carry

        lax.fori_loop(0, 18, gates, 0, unroll=2)

        for part in range(2):
            pltpu.make_async_copy(outgoing[part].at[0], incoming[part].at[0], own_sem.at[2 * u + part]).wait()

        def gather(group, carry):
            for part in range(2):
                arrival = recv_sem.at[(2 * u + part) * 8 + group]

                @pl.when(group == 0)
                def _():
                    blocks = incoming[part].at[pl.ds(0, 15)]
                    pltpu.make_async_copy(blocks, blocks, arrival).wait()

                @pl.when(group > 0)
                def _():
                    blocks = incoming[part].at[pl.ds(0, 16)]
                    pltpu.make_async_copy(blocks, blocks, arrival).wait()

            from_y, from_z = add_mod(y_lo, group, 2), add_mod(z_lo, lax.div(group, 2), 2)
            from_core = add_mod(core, lax.div(group, 4), 2)
            column = from_y * 4 + from_z * 2 + from_core
            for h in range(2):
                for hi in range(2):
                    for part in range(2):
                        turned = turn(
                            [incoming[part][(hi * 4 + at) * 16 + h * 8 + column].astype(F32) for at in range(4)]
                        )
                        for quarter in range(4):
                            for left_at, right_at, third, first, count in SEGMENTS[part]:
                                lanes = pl.ds((hi * 3 + third) * 128, 128)
                                to = pl.ds(h * 64 + quarter * 16 + first, count)
                                slab_left[to, lanes] = turned[quarter][left_at : left_at + count]
                                slab_right[to, lanes] = turned[quarter][right_at : right_at + count]
            if u == 0:
                left16[group] = slab_left[...].astype(BF16)
                for hi in range(2):
                    for third in range(3):
                        lanes = pl.ds((hi * 3 + third) * 128, 128)
                        flipped = slab_right[:, lanes].T
                        for at in range(4):
                            now, end = third * 32, third * 32 + 32
                            while now < end:
                                twelfth, within = now // 12, now % 12
                                count = min(12 - within, end - now)
                                to = (hi * 4 + at) * 128 + twelfth * 16 + within
                                source = at * 32 + now - third * 32
                                flipped_rows[to : to + count, :] = flipped[source : source + count]
                                now += count
                right_t[:, pl.ds(pl.multiple_of(group * 128, 128), 128)] = flipped_rows[...].astype(BF16)
            else:
                for h in range(2):
                    right16[h * 8 + column] = slab_right[h * 64 : h * 64 + 64, :].astype(BF16)
                    for quarter in range(4):
                        at = h * 64 + quarter * 16
                        compact[h, quarter * 12 : quarter * 12 + 12, :] = slab_left[at : at + 12, :]
                    for part in range(3):
                        sixth = from_core * 3 + part
                        to = h * 384 + lax.div(sixth, 2) * 128 + (from_y * 2 + from_z) * 32 + lax.rem(sixth, 2) * 16
                        left16.reshape(1024, 768)[pl.ds(pl.multiple_of(to, 16), 16), :] = compact[
                            h, part * 16 : part * 16 + 16, :
                        ].astype(BF16)
            return carry

        lax.fori_loop(0, 8, gather, 0)

        if u == 1:
            for part in range(2):
                pltpu.make_async_copy(
                    sums_out[part].at[others], sums_out[part].at[others], sums_send_sem.at[part]
                ).wait()

        def columns_of(step):
            turn_y = lax.div(step, 2)
            late = lax.div(turn_y, 2)
            to_y = add_mod(y, (1 - late) * (2 - 2 * turn_y) + late * (2 * turn_y - 3) + 2 * core, 4)
            return to_y * 2 + add_mod(z_lo, step, 2)

        def multiply(step, summed):
            rows_at = pl.ds(pl.multiple_of(columns_of(step) * 128, 128), 128)
            if u == 0:
                summed[...] = jnp.dot(
                    right_t[rows_at, :], left16.reshape(1024, 768)[...], preferred_element_type=F32
                )
            else:
                summed[...] = lax.dot_general(
                    right16.reshape(1024, 768)[rows_at, :], left16.reshape(1024, 768)[0:768, :],
                    (((1,), (1,)), ((), ())), preferred_element_type=F32,
                )

        def send_back(step, part):
            pair_at = columns_of(step)

            def one(member, carry):
                to_x = add_mod(x, offset_along(member, lax.div(step, 7) * part), 4)
                to_row = add_mod(z_hi, member, 2) * 4 + to_x
                s = pair_at * 2 + add_mod(core, lax.div(member, 2), 2)
                to = to_row * 16 + s

                def remote():
                    pltpu.make_async_remote_copy(
                        src_ref=sums_out[part].at[to], dst_ref=sums_in[part].at[my_channel],
                        send_sem=sums_send_sem.at[2 * u + part], recv_sem=sums_sem.at[2 * u + part],
                        device_id=(to_row, s), device_id_type=MESH,
                    ).start()

                if isinstance(member, int):
                    pl.when(to != me)(remote)

                    @pl.when(to == me)
                    def _():
                        pltpu.make_async_copy(
                            sums_out[part].at[to], sums_in[part].at[my_channel], own_sums_sem.at[2 * u + part]
                        ).start()
                else:
                    remote()
                return carry

            one(0, 0)
            lax.fori_loop(1, 16, one, 0, unroll=15)

        def spread(step, part, summed):
            for to_core in range(2):
                s = columns_of(step) * 2 + to_core
                for hi in range(2):
                    blocks = []
                    for quarter in range(4):
                        at = to_core * 64 + quarter * 16
                        pieces = [
                            summed[pl.ds(at + first, count), pl.ds((hi * 3 + third) * 128, 128)]
                            for _, _, third, first, count in SEGMENTS[part]
                        ]
                        blocks.append(jnp.concatenate(pieces, axis=0))
                    turned = turn(blocks)
                    for at in range(4):
                        to = (hi * 4 + at) * 16 + s
                        if part == 0:
                            sums_out0[to] = turned[at].astype(BF16)
                        else:
                            for four in range(5):
                                sums_out1[to, four] = turned[at][four * 4 : four * 4 + 4].astype(BF16)

        def give_first(steps, carry):
            spread(steps * 2, 0, summed0.at[steps])
            multiply(steps * 2 + 1, summed1.at[steps])
            send_back(steps * 2, 0)
            spread(steps * 2 + 1, 0, summed1.at[steps])
            multiply(lax.rem(steps * 2 + 2, 8), summed0.at[lax.rem(steps + 1, 4)])
            send_back(steps * 2 + 1, 0)
            return carry

        def give_rest(steps, carry):
            for parity, summed in enumerate((summed0, summed1)):
                spread(steps * 2 + parity, 1, summed.at[steps])
                send_back(steps * 2 + parity, 1)
            return carry

        multiply(0, summed0.at[0])
        lax.fori_loop(0, 4, give_first, 0)
        lax.fori_loop(0, 4, give_rest, 0)

        for part in range(2):
            pltpu.make_async_copy(
                outgoing[part].at[others], outgoing[part].at[others], send_sem.at[2 * u + part]
            ).wait()

        def widen(part):
            pltpu.make_async_copy(
                sums_out[part].at[0], sums_in[part].at[0], own_sums_sem.at[2 * u + part]
            ).wait()
            pltpu.make_async_copy(
                sums_in[part].at[others], sums_in[part].at[others], sums_sem.at[2 * u + part]
            ).wait()

            def one(channel, carry):
                to = channel * WIDE + FIRST_ROW[part]
                if part == 0:
                    widened[pl.ds(to, 16), :] = sums_in0[channel].astype(F32)
                else:
                    for four in range(5):
                        widened[pl.ds(to + four * 4, 4), :] = sums_in1[channel, four].astype(F32)
                return carry

            lax.fori_loop(0, DEVICES, one, 0, unroll=8)

        def finish(pair_of, carry):
            mixed = []
            for half in range(2):
                values = widened[pl.ds(pair_of * 2 + half, 128, stride=WIDE), :]
                mixed.append(norm_columns(values, columns[u, 2], columns[u, 3]))
            update = jnp.dot(out_t[u], jnp.concatenate(mixed, axis=1), preferred_element_type=F32)
            halves = []
            for half in range(2):
                tile = pair_of * 2 + half
                values = state[tile] + gate[tile] * update[:, half * 128 : half * 128 + 128]
                if u == 0:
                    state[tile] = values
                    halves.append(norm_columns(values, columns[1, 0], columns[1, 1]))
                else:
                    tokens = values.T
                    for q in range(4):
                        rows[token_rows(tile, q), :] = tokens[q * 32 : q * 32 + 32]
            if u == 0:
                normed[pair_of] = jnp.concatenate(halves, axis=1)
            return carry

        widen(0)
        if u == 0:
            lax.fori_loop(0, 8, finish, 0, unroll=2)
            project_and_send(1, 0)
            widen(1)
            lax.fori_loop(8, 18, finish, 0, unroll=2)
            project_and_send(1, 1)
        else:
            stores = [
                pltpu.make_async_copy(
                    rows.at[pl.ds(i * 1536, 1536)], out.at[pl.ds(i * 1536, 1536)], copy_sem.at[i]
                )
                for i in range(3)
            ]
            lax.fori_loop(0, 8, finish, 0, unroll=2)
            widen(1)
            lax.fori_loop(8, 14, finish, 0, unroll=2)
            stores[0].start()
            lax.fori_loop(14, 16, finish, 0, unroll=2)
            stores[1].start()
            lax.fori_loop(16, 18, finish, 0, unroll=2)
            stores[2].start()

    for part in range(2):
        pltpu.make_async_copy(
            sums_out[part].at[others], sums_out[part].at[others], sums_send_sem.at[2 + part]
        ).wait()
    for store in stores:
        store.wait()


def local(pair, *parameters):
    anywhere = pl.BlockSpec(memory_space=pl.ANY)
    done = pl.pallas_call(
        kernel,
        out_shape=jax.ShapeDtypeStruct((4608, 128), F32),
        in_specs=[anywhere] * 8,
        out_specs=anywhere,
        scratch_shapes=[pltpu.VMEM(p.shape, p.dtype) for p in parameters] + [
            pltpu.VMEM((4608, 128), F32),
            pltpu.VMEM((36, 128, 128), F32),
            pltpu.VMEM((36, 128, 128), F32),
            pltpu.VMEM((18, 128, 256), BF16),
            pltpu.VMEM((16 * STRIDE + 8, 128), F32),
            pltpu.VMEM((128 * WIDE, 128), F32),
            pltpu.VMEM((128, 32, 128), BF16),
            pltpu.VMEM((128, 40, 128), BF16),
            pltpu.VMEM((128, 32, 128), BF16),
            pltpu.VMEM((128, 40, 128), BF16),
            pltpu.VMEM((128, 16, 128), BF16),
            pltpu.VMEM((128, 5, 4, 128), BF16),
            pltpu.VMEM((128, 16, 128), BF16),
            pltpu.VMEM((128, 5, 4, 128), BF16),
            pltpu.VMEM((128, 768), F32),
            pltpu.VMEM((128, 768), F32),
            pltpu.VMEM((1024, 128), F32),
            pltpu.VMEM((2, 48, 768), F32),
            pltpu.VMEM((8, 128, 768), BF16),
            pltpu.VMEM((16, 64, 768), BF16),
            pltpu.VMEM((1024, 1024), BF16),
            pltpu.VMEM((4, 128, 768), F32),
            pltpu.VMEM((4, 128, 768), F32),
            pltpu.VMEM((2, 8, 64, 128), BF16),
            pltpu.VMEM((2, 128, 128), BF16),
            pltpu.VMEM((2, 128, 128), BF16),
            pltpu.VMEM((2, 4, 128, 128), F32),
            pltpu.SemaphoreType.DMA((3,)),
            pltpu.SemaphoreType.DMA((7,)),
            pltpu.SemaphoreType.DMA((4,)),
            pltpu.SemaphoreType.DMA((4,)),
            pltpu.SemaphoreType.DMA((4,)),
            pltpu.SemaphoreType.DMA((4,)),
            pltpu.SemaphoreType.DMA((32,)),
            pltpu.SemaphoreType.DMA((4,)),
            pltpu.SemaphoreType.REGULAR,
        ],
        compiler_params=pltpu.CompilerParams(
            collective_id=0, has_side_effects=True, vmem_limit_bytes=56 * 2**20
        ),
    )(pair.reshape(4608, 128), *parameters)
    return done.reshape(96, 48, 128)


def solution(mesh):
    return jax.shard_map(
        local,
        mesh=mesh,
        in_specs=(P("row", "col", None), P(), P(), P(), P(), P(), P(), P()),
        out_specs=P("row", "col", None),
        check_vma=False,
    )
```
